128 devices in a mesh: row: 16 (over y, z), col: 8 (over x, core).
Axes of the slice: x: 4, y: 4, z: 4, core: 2. Of those that a mesh axis runs over, the one named last changes fastest.
Arguments:
- spectrum_noise: float32 [2, 8192, 8192], P(None, ('row', 'col')), may hold values from -6 to 6
- power_spectrum: float32 [8192, 8192], P(('row', 'col')), may hold values from 0.1 to 10
- site_block: int32 [16384], P(('row', 'col')), may hold values from 0 to 127, as said below
- site_cell: int32 [2, 16384], P(None, ('row', 'col')), may hold values from 0 to 8191, as said below
- site_frac: float32 [2, 16384], P(None, ('row', 'col')), may hold values from 0 to 1
Outputs:
- field: float32 [2, 8192, 8192], P(None, ('row', 'col'))
- samples: float32 [2, 16384], P(None, ('row', 'col'))
The draws below stay inside these ranges and needn't reach their ends.
Inputs may be any that keep to these rules, and one draw needn't show every extreme that they name: `site_block`: no row block holds more than 2 stations of one device, and every device has exactly 2 stations in some block. Every row block holds a station of the device of the same index, in the block's last row. `site_cell`: the first row is below 64.
All inputs are finite; a program needn't handle non-finite values.
Results may differ from the reference program's by a relative error of at most 0.00008.
Values sent between devices are 32-bit elements; how exact they have to be, the bound alone decides.
No kernel may reach another device: no remote copies, remote signals or barrier semaphores. Data moves between devices by JAX's collectives and lax.ppermute only.
A program may use at most 128 MiB of HBM per device.

```python
import math
import jax
import jax.numpy as jnp
from jax import lax

GRID = 8192
SITES_DEV = 128
CAP = 2
ROWS = 64
SITES = 16384


def site_layout(key):
    spread = SITES_DEV // CAP
    devices = SITES // SITES_DEV
    stride = devices // spread
    key_hot, key_pull = jax.random.split(key)
    hotspot = jax.random.randint(key_hot, (), 0, devices)
    pull_back = jax.random.randint(key_pull, (devices,), 0, spread - 2)
    device = jnp.arange(devices, dtype=jnp.int32)
    offset = 1 + jnp.minimum((device - hotspot) % devices, pull_back)
    position = jnp.arange(SITES_DEV, dtype=jnp.int32)
    group = position[None, :] // CAP
    relative = group - offset[:, None]
    moved = jnp.where(jnp.abs(relative) <= 1, relative, relative * stride)
    block_id = (device[:, None] + moved) % devices
    last_row = position[None, :] == CAP * offset[:, None]
    return (block_id.reshape(-1).astype(jnp.int32), last_row.reshape(-1))


def draw_site_block(key, part):
    block_id, last_row = site_layout(key)
    return block_id


def draw_site_cell(key, part):
    block_id, last_row = site_layout(key)
    key = jax.random.fold_in(key, 12)
    key_row, key_col = jax.random.split(key)
    row_local = jax.random.randint(key_row, (SITES,), 0, ROWS)
    row_local = jnp.where(last_row, ROWS - 1, row_local)
    column = jax.random.randint(key_col, (SITES,), 0, GRID)
    return jnp.stack([row_local, column]).astype(jnp.int32)


def steps_of(own_key, shape, cuts, low, top_value):
    def one(axis_at, blocks):
        heights = jax.random.uniform(jax.random.fold_in(jax.random.fold_in(own_key, 6), axis_at), (blocks,), jnp.float32, low / len(cuts), top_value / len(cuts))
        return jnp.repeat(jnp.exp(heights), shape[axis_at] // blocks).reshape((-1,) + (1,) * (len(shape) - axis_at - 1))

    gain = one(*cuts[0])
    for cut in cuts[1:]:
        gain = gain * one(*cut)
    return gain


def noise(rng, extent, scale, reach, pieces=(), held_as=jnp.bfloat16):
    factor_of = steps_of(rng, extent, pieces, -0.22, 0.18) if pieces else 1.0
    array = jax.random.normal(rng, extent, jnp.float32) * scale * factor_of
    return jnp.minimum(jnp.maximum(array, -reach), reach).astype(held_as)


def setup_inputs(seed: int = 0) -> dict:
    seeds = jax.random.split(jax.random.key(seed), 6)
    spectrum_noise = noise(seeds[0], (2, GRID, GRID), 1.0, 6.0, ((1, 128),), jnp.float32)
    power_spectrum = jnp.clip(jnp.exp(math.log(10.0) - 4.6051702 * jax.random.uniform(seeds[1], (GRID, GRID), jnp.float32) ** steps_of(seeds[1], (GRID, GRID), ((0, 128),), -0.2, 0.2)), 0.1, 10.0)
    site_block = draw_site_block(jax.random.fold_in(seeds[5], 71), 0)
    site_cell = draw_site_cell(jax.random.fold_in(seeds[5], 71), 0)
    site_frac = jnp.clip(1.0 * jax.random.uniform(seeds[4], (2, SITES), jnp.float32) ** steps_of(seeds[4], (2, SITES), ((1, 128),), -0.2, 0.2), 0.0, 1.0)
    return dict(spectrum_noise=spectrum_noise, power_spectrum=power_spectrum, site_block=site_block, site_cell=site_cell, site_frac=site_frac)


def reference(spectrum_noise, power_spectrum, site_block, site_cell, site_frac):
    amplitude = jnp.sqrt(power_spectrum)
    spectrum = lax.complex(amplitude * spectrum_noise[0], amplitude * spectrum_noise[1])
    flipped = jnp.fft.ifft2(spectrum) * GRID
    flat_field = flipped.reshape(-1)
    row_lo = site_block.astype(jnp.int32) * ROWS + site_cell[0].astype(jnp.int32)
    col_lo = site_cell[1].astype(jnp.int32)
    row_hi = (row_lo + 1) % GRID
    col_hi = (col_lo + 1) % GRID

    def pick(row_at, col_at):
        return flat_field[col_at * GRID + row_at]
    row_frac = site_frac[0]
    col_frac = site_frac[1]
    value = (1 - row_frac) * (1 - col_frac) * pick(row_lo, col_lo) + (1 - row_frac) * col_frac * pick(row_lo, col_hi) + row_frac * (1 - col_frac) * pick(row_hi, col_lo) + row_frac * col_frac * pick(row_hi, col_hi)
    samples = jnp.stack([jnp.real(value), jnp.imag(value)]).astype(jnp.float32)
    turned = flipped.T
    field = jnp.stack([jnp.real(turned), jnp.imag(turned)]).astype(jnp.float32)
    return (field, samples)
```

```python
import numpy as np
import ml_dtypes
import jax
import jax.numpy as jnp
from jax import lax
from jax.experimental import pallas as pl
from jax.experimental.pallas import tpu as pltpu
from jax.sharding import PartitionSpec as P

GRID = 8192
DEVICES = 128
ROWS = 64
MESSAGE = 65
AXES = ("row", "col")
VMEM = pl.BlockSpec(memory_space=pltpu.VMEM)
HIGH = lax.Precision.HIGHEST
LAST = (((1,), (1,)), ((), ()))


def phase(product, length):
    angle = 2.0 * np.pi / length * (product % length)
    return np.cos(angle), np.sin(angle)


def complex_matrix(cosine, sine):
    return np.block([[cosine, -sine], [sine, cosine]])


def split_table(table):
    high = table.astype(ml_dtypes.bfloat16)
    low = (table - high.astype(np.float64)).astype(ml_dtypes.bfloat16)
    return high, low


def make_tables():
    short, long = np.arange(64), np.arange(128)
    high, low = split_table(complex_matrix(*phase(np.outer(short, short), 64)))
    short_first = np.block([[high, high], [low, np.zeros_like(low)]])
    turn_first = np.stack(phase(np.outer(short, long), GRID)).astype(np.float32)
    long_both = np.stack(split_table(complex_matrix(*phase(np.outer(long, long), 128))))
    turn_second = np.stack(phase(np.outer(long, short), GRID)) / GRID
    turn_second = np.concatenate([turn_second, turn_second], axis=2).astype(np.float32)
    cosine, sine = phase(np.outer(short, short), 64)
    pair = np.eye(2)
    short_second = np.stack(
        split_table(complex_matrix(np.kron(pair, cosine), np.kron(pair, sine)))
    )
    return short_first, turn_first, long_both, turn_second, short_second


def split(value):
    high = value.astype(jnp.bfloat16)
    low = (value - high.astype(jnp.float32)).astype(jnp.bfloat16)
    return high, low


def dot(left, right, dims=(((1,), (0,)), ((), ()))):
    return lax.dot_general(left, right, dims, preferred_element_type=jnp.float32)


def split_dot(table, value, dims=(((1,), (0,)), ((), ()))):
    high, low = split(value)
    return dot(table[0], high, dims) + dot(table[0], low, dims) + dot(table[1], high, dims)


def site_slots(block):
    wide = jnp.broadcast_to(block.astype(jnp.float32), (DEVICES, DEVICES))
    before = lax.broadcasted_iota(jnp.int32, (DEVICES, DEVICES), 0)
    after = lax.broadcasted_iota(jnp.int32, (DEVICES, DEVICES), 1)
    earlier = (wide == wide.T) & (before < after)
    return jnp.sum(jnp.where(earlier, 1.0, 0.0), axis=0, keepdims=True)


def site_requests(block, cell, frac):
    slot = site_slots(block)
    row, column = cell[0:1], cell[1:2]
    column_next = (column + 1) & (GRID - 1)
    part_row, part_col = frac[0:1], frac[1:2]
    edge = row == ROWS - 1
    row_next = jnp.where(edge, row, row + 1)

    def line(field_row, field_col):
        return ((field_row >> 3) * 512 + (field_col >> 7) * 8 + (field_row & 7)).astype(jnp.float32)

    lane = (column & 127).astype(jnp.float32)
    lane_next = (column_next & 127).astype(jnp.float32)
    lower = jnp.where(edge, 0.0, part_row)
    zero = jnp.zeros_like(row)
    own = [
        line(row, column),
        line(row, column_next),
        line(row_next, column),
        line(row_next, column_next),
        lane,
        lane_next,
        (1 - part_row) * (1 - part_col),
        (1 - part_row) * part_col,
        lower * (1 - part_col),
        lower * part_col,
    ]
    halo = [
        line(zero, column),
        line(zero, column_next),
        lane,
        lane_next,
        part_row * (1 - part_col),
        part_row * part_col,
    ]
    blank = jnp.zeros((1, DEVICES), jnp.float32)
    groups = []
    for at, values in ((0, own), (10, own), (20, halo), (26, halo)):
        lines = [blank] * at + values
        groups.append(jnp.concatenate(lines + [blank] * (DEVICES - len(lines)), axis=0))
    owner = lax.broadcasted_iota(jnp.int32, (DEVICES, DEVICES), 0)
    here = owner == block
    below = (owner == ((block + 1) & (DEVICES - 1))) & edge
    picks = []
    for mask in (here, below):
        for which in (0.0, 1.0):
            picks.append(jnp.where(mask & (slot == which), 1.0, 0.0))
    return lax.dot_general(
        jnp.concatenate(picks, axis=1),
        jnp.concatenate(groups, axis=1),
        LAST,
        precision=HIGH,
        preferred_element_type=jnp.float32,
    )


def first_kernel(
    noise_hbm,
    power_hbm,
    block_ref,
    cell_ref,
    frac_ref,
    short_ref,
    turn_ref,
    long_ref,
    out_ref,
    noise,
    power,
    middle,
    noise_sem,
    power_sem,
):
    copies = []
    for i in range(8):
        copies.append(
            (
                pltpu.make_async_copy(noise_hbm.at[:, i], noise.at[:, i], noise_sem.at[i]),
                pltpu.make_async_copy(power_hbm.at[i], power.at[i], power_sem.at[i]),
            )
        )
        copies[-1][0].start()
        copies[-1][1].start()
    out_ref[pl.ds(MESSAGE - 1, DEVICES, stride=MESSAGE), :] = site_requests(
        block_ref[...], cell_ref[...], frac_ref[...]
    )
    for i in range(8):
        copies[i][0].wait()
        copies[i][1].wait()

        def rows(pair, carry, i=i):
            parts = []
            for k in range(2):
                at = pl.ds(2 * pair + k, 64, stride=8)
                amplitude = jnp.sqrt(power[i, at, :])
                stacked = jnp.concatenate(
                    [amplitude * noise[0, i, at, :], amplitude * noise[1, i, at, :]], axis=0
                )
                parts.append(jnp.concatenate(split(stacked), axis=0))
            sums = dot(short_ref[...], jnp.concatenate(parts, axis=1))
            sums = sums[:128] + sums[128:]
            for k in range(2):
                real = sums[:64, 128 * k : 128 * k + 128]
                imag = sums[64:, 128 * k : 128 * k + 128]
                at = pl.ds(8 * i + 2 * pair + k, 64, stride=64)
                middle[0, at, :] = real * turn_ref[0] - imag * turn_ref[1]
                middle[1, at, :] = real * turn_ref[1] + imag * turn_ref[0]
            return carry

        lax.fori_loop(0, 4, rows, 0, unroll=True)

    def columns(step, carry):
        at = pl.ds(pl.multiple_of(256 * step, 256), 256)
        value = jnp.concatenate([middle[0, at, :], middle[1, at, :]], axis=1)
        sums = split_dot(long_ref, value, LAST)
        for part in range(2):
            for k in range(2):
                j = 32 * part + 2 * step + k
                out_ref[pl.ds(j, DEVICES, stride=MESSAGE), :] = sums[
                    128 * part : 128 * part + 128, 128 * k : 128 * k + 128
                ]
        return carry

    lax.fori_loop(0, 16, columns, 0, unroll=4)


def second_kernel(
    got_ref,
    long_ref,
    turn_ref,
    short_ref,
    field_hbm,
    answer_ref,
    field,
    picked,
    code_vmem,
    code_smem,
    field_sem,
    code_sem,
):
    asked = got_ref[pl.ds(MESSAGE - 1, DEVICES, stride=MESSAGE), :]
    code_vmem[...] = (asked + 0.5).astype(jnp.int32)
    code_copy = pltpu.make_async_copy(code_vmem, code_smem, code_sem)
    code_copy.start()
    copies = []
    for i in range(8):
        for half in range(2):
            pair = 4 * i + 2 * half
            value = jnp.concatenate(
                [
                    jnp.concatenate(
                        [
                            got_ref[pl.ds(32 * part + pair + k, DEVICES, stride=MESSAGE), :]
                            for k in range(2)
                        ],
                        axis=1,
                    )
                    for part in range(2)
                ],
                axis=0,
            )
            sums = split_dot(long_ref, value)
            turned = []
            for k in range(2):
                real = sums[:128, 128 * k : 128 * k + 128]
                imag = sums[128:, 128 * k : 128 * k + 128]
                turned.append(
                    jnp.concatenate(
                        [
                            real * turn_ref[0] - imag * turn_ref[1],
                            real * turn_ref[1] + imag * turn_ref[0],
                        ],
                        axis=1,
                    )
                )
            sums = split_dot(short_ref, jnp.concatenate(turned, axis=0), LAST)
            for part in range(2):
                for odd in range(2):
                    for k in range(2):
                        top = 128 * part + 64 * odd
                        at = pl.ds(512 * i + 4 * half + 2 * k + odd, 64, stride=8)
                        field[part, at, :] = sums[top : top + 64, 128 * k : 128 * k + 128]
        span = pl.ds(512 * i, 512)
        copies.append(
            pltpu.make_async_copy(field.at[:, span], field_hbm.at[:, span], field_sem.at[i])
        )
        copies[-1].start()
    code_copy.wait()

    def gather(device, carry):
        for which in range(2):
            for k in range(6):
                lane = 10 * which + k if k < 4 else 20 + 6 * which + k - 4
                line = code_smem[device, lane]
                for part in range(2):
                    picked[which, part, k, pl.ds(device, 1), :] = field[part, pl.ds(line, 1), :]
        return carry

    lax.fori_loop(0, DEVICES, gather, 0, unroll=4)
    lanes = lax.broadcasted_iota(jnp.int32, (DEVICES, 128), 1).astype(jnp.float32)
    answer = jnp.zeros((DEVICES, 128), jnp.float32)
    for which in range(2):
        own, halo = 10 * which, 20 + 6 * which

        def column(at):
            return asked[:, at : at + 1]

        first = lanes == column(own + 4)
        second = lanes == column(own + 5)
        halo_first = lanes == column(halo + 2)
        halo_second = lanes == column(halo + 3)
        for part in range(2):
            left = column(own + 6) * picked[which, part, 0] + column(own + 8) * picked[which, part, 2]
            right = column(own + 7) * picked[which, part, 1] + column(own + 9) * picked[which, part, 3]
            value = jnp.where(first, left, 0.0) + jnp.where(second, right, 0.0)
            edge = jnp.where(halo_first, column(halo + 4) * picked[which, part, 4], 0.0)
            edge += jnp.where(halo_second, column(halo + 5) * picked[which, part, 5], 0.0)
            answer = jnp.where(
                lanes == 2 * which + part, jnp.sum(value, axis=1, keepdims=True), answer
            )
            answer = jnp.where(
                lanes == 4 + 2 * which + part, jnp.sum(edge, axis=1, keepdims=True), answer
            )
    answer_ref[...] = answer
    for copy in copies:
        copy.wait()


def last_kernel(answer_ref, block_ref, cell_ref, out_ref):
    block = block_ref[...]
    slot = site_slots(block)
    edge = cell_ref[0:1] == ROWS - 1
    owner = lax.broadcasted_iota(jnp.int32, (DEVICES, DEVICES), 0)
    values = answer_ref[...].T[:8]

    def pick(mask):
        return jnp.dot(
            values,
            jnp.where(mask, 1.0, 0.0),
            precision=HIGH,
            preferred_element_type=jnp.float32,
        )

    here = pick(owner == block)
    below = pick(owner == ((block + 1) & (DEVICES - 1)))
    own = jnp.where(slot == 0.0, here[0:2], here[2:4])
    halo = jnp.where(slot == 0.0, below[4:6], below[6:8])
    out_ref[...] = own + jnp.where(edge, halo, 0.0)


def exchange(value):
    return lax.all_to_all(value, AXES, split_axis=0, concat_axis=0, tiled=True)


def per_device(spectrum_noise, power_spectrum, site_block, site_cell, site_frac):
    short_first, turn_first, long_both, turn_second, short_second = make_tables()
    any_space = pl.BlockSpec(memory_space=pl.ANY)
    noise = spectrum_noise.reshape(2, 8, 8, 64, 128).transpose(0, 1, 3, 2, 4).reshape(2, 8, 512, 128)
    power = power_spectrum.reshape(8, 8, 64, 128).transpose(0, 2, 1, 3).reshape(8, 512, 128)
    block = site_block.reshape(1, DEVICES)
    sent = pl.pallas_call(
        first_kernel,
        out_shape=jax.ShapeDtypeStruct((DEVICES * MESSAGE, 128), jnp.float32),
        in_specs=[any_space, any_space] + [VMEM] * 6,
        out_specs=VMEM,
        scratch_shapes=[
            pltpu.VMEM((2, 8, 512, 128), jnp.float32),
            pltpu.VMEM((8, 512, 128), jnp.float32),
            pltpu.VMEM((2, 4096, 128), jnp.float32),
            pltpu.SemaphoreType.DMA((8,)),
            pltpu.SemaphoreType.DMA((8,)),
        ],
        compiler_params=pltpu.CompilerParams(vmem_limit_bytes=40 << 20),
        name="first_pass",
    )(noise, power, block, site_cell, site_frac, short_first, turn_first, long_both)
    got = exchange(sent.reshape(DEVICES * MESSAGE, 1, 128)).reshape(DEVICES * MESSAGE, 128)
    field, answer = pl.pallas_call(
        second_kernel,
        out_shape=(
            jax.ShapeDtypeStruct((2, 4096, 128), jnp.float32),
            jax.ShapeDtypeStruct((DEVICES, 128), jnp.float32),
        ),
        in_specs=[VMEM] * 4,
        out_specs=(any_space, VMEM),
        scratch_shapes=[
            pltpu.VMEM((2, 4096, 128), jnp.float32),
            pltpu.VMEM((2, 2, 6, DEVICES, 128), jnp.float32),
            pltpu.VMEM((DEVICES, 128), jnp.int32),
            pltpu.SMEM((DEVICES, 128), jnp.int32),
            pltpu.SemaphoreType.DMA((8,)),
            pltpu.SemaphoreType.DMA,
        ],
        compiler_params=pltpu.CompilerParams(vmem_limit_bytes=40 << 20),
        name="second_pass",
    )(got, long_both, turn_second, short_second)
    back = exchange(answer.reshape(DEVICES, 1, 128)).reshape(DEVICES, 128)
    samples = pl.pallas_call(
        last_kernel,
        out_shape=jax.ShapeDtypeStruct((2, DEVICES), jnp.float32),
        in_specs=[VMEM] * 3,
        out_specs=VMEM,
        name="samples",
    )(back, block, site_cell)
    field = field.reshape(2, 8, 64, 8, 128).transpose(0, 1, 3, 2, 4).reshape(2, ROWS, GRID)
    return field, samples


def solution(mesh):
    return jax.shard_map(
        per_device,
        mesh=mesh,
        in_specs=(
            P(None, AXES, None),
            P(AXES, None),
            P(AXES),
            P(None, AXES),
            P(None, AXES),
        ),
        out_specs=(P(None, AXES, None), P(None, AXES)),
        check_vma=False,
    )
```

```python
import numpy as np
import ml_dtypes
import jax
import jax.numpy as jnp
from jax import lax
from jax.experimental import pallas as pl
from jax.experimental.pallas import tpu as pltpu
from jax.sharding import PartitionSpec as P

GRID = 8192
DEVICES = 128
ROWS = 64
MESSAGE = 65
PITCH = 72
CHUNKS = ((0, 1), (1, 1), (2, 2), (4, 4))
AXES = ("row", "col")
VMEM = pl.BlockSpec(memory_space=pltpu.VMEM)
HIGH = lax.Precision.HIGHEST
LAST = (((1,), (1,)), ((), ()))


def phase(product, length):
    angle = 2.0 * np.pi / length * (product % length)
    return np.cos(angle), np.sin(angle)


def complex_matrix(cosine, sine):
    return np.block([[cosine, -sine], [sine, cosine]])


def split_table(table):
    high = table.astype(ml_dtypes.bfloat16)
    low = (table - high.astype(np.float64)).astype(ml_dtypes.bfloat16)
    return high, low


def make_tables():
    short, long = np.arange(64), np.arange(128)
    high, low = split_table(complex_matrix(*phase(np.outer(short, short), 64)))
    short_first = np.block([[high, high], [low, np.zeros_like(low)]])
    turn_first = np.stack(phase(np.outer(short, long), GRID)).astype(np.float32)
    long_both = np.stack(split_table(complex_matrix(*phase(np.outer(long, long), 128))))
    turn_second = np.stack(phase(np.outer(long, short), GRID)) / GRID
    turn_second = np.concatenate([turn_second, turn_second], axis=2).astype(np.float32)
    cosine, sine = phase(np.outer(short, short), 64)
    pair = np.eye(2)
    short_second = np.stack(
        split_table(complex_matrix(np.kron(pair, cosine), np.kron(pair, sine)))
    )
    return short_first, turn_first, long_both, turn_second, short_second


def split(value):
    high = value.astype(jnp.bfloat16)
    low = (value - high.astype(jnp.float32)).astype(jnp.bfloat16)
    return high, low


def dot(left, right, dims=(((1,), (0,)), ((), ()))):
    return lax.dot_general(left, right, dims, preferred_element_type=jnp.float32)


def split_dot(table, value, dims=(((1,), (0,)), ((), ()))):
    high, low = split(value)
    return dot(table[0], high, dims) + dot(table[0], low, dims) + dot(table[1], high, dims)


def site_slots(block):
    wide = jnp.broadcast_to(block.astype(jnp.float32), (DEVICES, DEVICES))
    before = lax.broadcasted_iota(jnp.int32, (DEVICES, DEVICES), 0)
    after = lax.broadcasted_iota(jnp.int32, (DEVICES, DEVICES), 1)
    earlier = (wide == wide.T) & (before < after)
    return jnp.sum(jnp.where(earlier, 1.0, 0.0), axis=0, keepdims=True)


def site_requests(block, cell, frac):
    slot = site_slots(block)
    row, column = cell[0:1], cell[1:2]
    column_next = (column + 1) & (GRID - 1)
    part_row, part_col = frac[0:1], frac[1:2]
    edge = row == ROWS - 1
    row_next = jnp.where(edge, row, row + 1)

    def line(field_row, field_col):
        return ((field_row >> 3) * 512 + (field_col >> 7) * 8 + (field_row & 7)).astype(jnp.float32)

    lane = (column & 127).astype(jnp.float32)
    lane_next = (column_next & 127).astype(jnp.float32)
    lower = jnp.where(edge, 0.0, part_row)
    zero = jnp.zeros_like(row)
    own = [
        line(row, column),
        line(row, column_next),
        line(row_next, column),
        line(row_next, column_next),
        lane,
        lane_next,
        (1 - part_row) * (1 - part_col),
        (1 - part_row) * part_col,
        lower * (1 - part_col),
        lower * part_col,
    ]
    halo = [
        line(zero, column),
        line(zero, column_next),
        lane,
        lane_next,
        part_row * (1 - part_col),
        part_row * part_col,
    ]
    blank = jnp.zeros((1, DEVICES), jnp.float32)
    groups = []
    for at, values in ((0, own), (10, own), (20, halo), (26, halo)):
        lines = [blank] * at + values
        groups.append(jnp.concatenate(lines + [blank] * (DEVICES - len(lines)), axis=0))
    owner = lax.broadcasted_iota(jnp.int32, (DEVICES, DEVICES), 0)
    here = owner == block
    below = (owner == ((block + 1) & (DEVICES - 1))) & edge
    picks = []
    for mask in (here, below):
        for which in (0.0, 1.0):
            picks.append(jnp.where(mask & (slot == which), 1.0, 0.0))
    return lax.dot_general(
        jnp.concatenate(picks, axis=1),
        jnp.concatenate(groups, axis=1),
        LAST,
        precision=HIGH,
        preferred_element_type=jnp.float32,
    )


def first_kernel(
    noise_hbm,
    power_hbm,
    block_hbm,
    cell_hbm,
    frac_hbm,
    short_hbm,
    turn_hbm,
    long_hbm,
    out_ref,
    noise,
    power,
    block_ref,
    cell_ref,
    frac_ref,
    short_ref,
    turn_ref,
    long_ref,
    middle,
    noise_sem,
    power_sem,
    small_sem,
):
    small = [
        pltpu.make_async_copy(source, target, small_sem.at[k])
        for k, (source, target) in enumerate(
            (
                (block_hbm, block_ref),
                (cell_hbm, cell_ref),
                (frac_hbm, frac_ref),
                (short_hbm, short_ref),
                (turn_hbm, turn_ref),
                (long_hbm, long_ref),
            )
        )
    ]
    large = []
    for k, (start, count) in enumerate(CHUNKS):
        span = pl.ds(start, count)
        large.append(
            (
                pltpu.make_async_copy(power_hbm.at[span], power.at[span], power_sem.at[k]),
                pltpu.make_async_copy(noise_hbm.at[:, span], noise.at[:, span], noise_sem.at[k]),
            )
        )
    for copy in small[:5] + list(large[0]) + small[5:]:
        copy.start()
    for pair in large[1:]:
        pair[0].start()
        pair[1].start()
    for copy in small[:3]:
        copy.wait()
    out_ref[pl.ds(MESSAGE - 1, DEVICES, stride=MESSAGE), :] = site_requests(
        block_ref[...], cell_ref[...], frac_ref[...]
    )
    small[3].wait()
    small[4].wait()
    for k, (start, count) in enumerate(CHUNKS):
        large[k][0].wait()
        large[k][1].wait()
        for first in range(8 * start, 8 * (start + count), 2):
            parts = []
            for row in (first, first + 1):
                at = pl.ds(row % 8, 64, stride=8)
                level = power[row // 8, at, :]
                amplitude = level * lax.rsqrt(level)
                stacked = jnp.concatenate(
                    [amplitude * noise[0, row // 8, at, :], amplitude * noise[1, row // 8, at, :]],
                    axis=0,
                )
                parts.append(jnp.concatenate(split(stacked), axis=0))
            sums = dot(short_ref[...], jnp.concatenate(parts, axis=1))
            sums = sums[:128] + sums[128:]
            for k2 in range(2):
                real = sums[:64, 128 * k2 : 128 * k2 + 128]
                imag = sums[64:, 128 * k2 : 128 * k2 + 128]
                at = pl.ds(first + k2, 64, stride=PITCH)
                middle[0, at, :] = real * turn_ref[0] - imag * turn_ref[1]
                middle[1, at, :] = real * turn_ref[1] + imag * turn_ref[0]
    small[5].wait()
    for step in range(16):
        value = jnp.concatenate(
            [
                jnp.concatenate(
                    [middle[part, pl.ds(PITCH * (4 * step + k), 64), :] for k in range(4)], axis=0
                )
                for part in range(2)
            ],
            axis=1,
        )
        sums = split_dot(long_ref, value, LAST)
        for part in range(2):
            for k in range(2):
                j = 32 * part + 2 * step + k
                out_ref[pl.ds(j, DEVICES, stride=MESSAGE), :] = sums[
                    128 * part : 128 * part + 128, 128 * k : 128 * k + 128
                ]


def second_kernel(
    got_ref,
    long_ref,
    turn_ref,
    short_ref,
    field_hbm,
    answer_ref,
    field,
    picked,
    code_vmem,
    code_smem,
    field_sem,
    code_sem,
):
    asked = got_ref[pl.ds(MESSAGE - 1, DEVICES, stride=MESSAGE), :]
    code_vmem[...] = (asked + 0.5).astype(jnp.int32)
    code_copy = pltpu.make_async_copy(code_vmem, code_smem, code_sem)
    code_copy.start()
    copies = []
    for i in range(8):
        for half in range(2):
            pair = 4 * i + 2 * half
            value = jnp.concatenate(
                [
                    jnp.concatenate(
                        [
                            got_ref[pl.ds(32 * part + pair + k, DEVICES, stride=MESSAGE), :]
                            for k in range(2)
                        ],
                        axis=1,
                    )
                    for part in range(2)
                ],
                axis=0,
            )
            sums = split_dot(long_ref, value)
            turned = []
            for k in range(2):
                real = sums[:128, 128 * k : 128 * k + 128]
                imag = sums[128:, 128 * k : 128 * k + 128]
                turned.append(
                    jnp.concatenate(
                        [
                            real * turn_ref[0] - imag * turn_ref[1],
                            real * turn_ref[1] + imag * turn_ref[0],
                        ],
                        axis=1,
                    )
                )
            sums = split_dot(short_ref, jnp.concatenate(turned, axis=0), LAST)
            for part in range(2):
                for odd in range(2):
                    for k in range(2):
                        top = 128 * part + 64 * odd
                        at = pl.ds(512 * i + 4 * half + 2 * k + odd, 64, stride=8)
                        field[part, at, :] = sums[top : top + 64, 128 * k : 128 * k + 128]
        span = pl.ds(512 * i, 512)
        copies.append(
            pltpu.make_async_copy(field.at[:, span], field_hbm.at[:, span], field_sem.at[i])
        )
        copies[-1].start()
    code_copy.wait()

    head = lax.broadcasted_iota(jnp.int32, (1, 128), 1) == 0

    def gather(device, carry):
        for which in range(2):
            for k in range(3):
                lane = 10 * which + 2 * k if k < 2 else 20 + 6 * which
                line = code_smem[device, lane]
                line_next = code_smem[device, lane + 1]
                for part in range(2):
                    picked[which, part, k, pl.ds(device, 1), :] = jnp.where(
                        head,
                        field[part, pl.ds(line_next, 1), :],
                        field[part, pl.ds(line, 1), :],
                    )
        return carry

    lax.fori_loop(0, DEVICES, gather, 0, unroll=8)
    lanes = lax.broadcasted_iota(jnp.int32, (DEVICES, 128), 1).astype(jnp.float32)
    answer = jnp.zeros((DEVICES, 128), jnp.float32)

    def column(at):
        return asked[:, at : at + 1]

    for which in range(2):
        own, halo = 10 * which, 20 + 6 * which

        def weights(lane, weight):
            return jnp.where(lanes == column(lane), column(weight), 0.0) + jnp.where(
                lanes == column(lane + 1), column(weight + 1), 0.0
            )

        upper = weights(own + 4, own + 6)
        lower = weights(own + 4, own + 8)
        edge = weights(halo + 2, halo + 4)
        for part in range(2):
            value = upper * picked[which, part, 0] + lower * picked[which, part, 1]
            answer = jnp.where(
                lanes == 2 * which + part, jnp.sum(value, axis=1, keepdims=True), answer
            )
            beyond = jnp.sum(edge * picked[which, part, 2], axis=1, keepdims=True)
            answer = jnp.where(lanes == 4 + 2 * which + part, beyond, answer)
    answer_ref[...] = answer
    for copy in copies:
        copy.wait()


def last_kernel(answer_ref, block_ref, cell_ref, out_ref):
    block = block_ref[...]
    slot = site_slots(block)
    edge = cell_ref[0:1] == ROWS - 1
    owner = lax.broadcasted_iota(jnp.int32, (DEVICES, DEVICES), 0)
    values = answer_ref[...].T[:8]
    masks = jnp.concatenate([owner == block, owner == ((block + 1) & (DEVICES - 1))], axis=1)
    high, middle = split(values)
    rest = values - high.astype(jnp.float32) - middle.astype(jnp.float32)
    terms = jnp.concatenate([high, middle, rest.astype(jnp.bfloat16)], axis=0)
    sums = dot(terms, jnp.where(masks, 1.0, 0.0).astype(jnp.bfloat16))
    sums = sums[0:8] + sums[8:16] + sums[16:24]
    here, below = sums[:, :DEVICES], sums[:, DEVICES:]
    own = jnp.where(slot == 0.0, here[0:2], here[2:4])
    halo = jnp.where(slot == 0.0, below[4:6], below[6:8])
    out_ref[...] = own + jnp.where(edge, halo, 0.0)


def exchange(value):
    return lax.all_to_all(value, AXES, split_axis=0, concat_axis=0, tiled=True)


def per_device(spectrum_noise, power_spectrum, site_block, site_cell, site_frac):
    short_first, turn_first, long_both, turn_second, short_second = make_tables()
    any_space = pl.BlockSpec(memory_space=pl.ANY)
    noise = spectrum_noise.reshape(2, 8, 8, 64, 128).transpose(0, 1, 3, 2, 4).reshape(2, 8, 512, 128)
    power = power_spectrum.reshape(8, 8, 64, 128).transpose(0, 2, 1, 3).reshape(8, 512, 128)
    block = site_block.reshape(1, DEVICES)
    operands = [
        pltpu.with_memory_space_constraint(operand, pltpu.HBM)
        for operand in map(
            jnp.asarray,
            (noise, power, block, site_cell, site_frac, short_first, turn_first, long_both),
        )
    ]
    sent = pl.pallas_call(
        first_kernel,
        out_shape=jax.ShapeDtypeStruct((DEVICES * MESSAGE, 128), jnp.float32),
        in_specs=[pl.BlockSpec(memory_space=pltpu.HBM)] * 8,
        out_specs=VMEM,
        scratch_shapes=[
            pltpu.VMEM((2, 8, 512, 128), jnp.float32),
            pltpu.VMEM((8, 512, 128), jnp.float32),
            pltpu.VMEM((1, DEVICES), jnp.int32),
            pltpu.VMEM((2, DEVICES), jnp.int32),
            pltpu.VMEM((2, DEVICES), jnp.float32),
            pltpu.VMEM((256, 256), jnp.bfloat16),
            pltpu.VMEM((2, 64, 128), jnp.float32),
            pltpu.VMEM((2, 256, 256), jnp.bfloat16),
            pltpu.VMEM((2, 64 * PITCH, 128), jnp.float32),
            pltpu.SemaphoreType.DMA((len(CHUNKS),)),
            pltpu.SemaphoreType.DMA((len(CHUNKS),)),
            pltpu.SemaphoreType.DMA((6,)),
        ],
        compiler_params=pltpu.CompilerParams(vmem_limit_bytes=40 << 20),
        name="first_pass",
    )(*operands)
    got = exchange(sent.reshape(DEVICES * MESSAGE, 1, 128)).reshape(DEVICES * MESSAGE, 128)
    field, answer = pl.pallas_call(
        second_kernel,
        out_shape=(
            jax.ShapeDtypeStruct((2, 4096, 128), jnp.float32),
            jax.ShapeDtypeStruct((DEVICES, 128), jnp.float32),
        ),
        in_specs=[VMEM] * 4,
        out_specs=(any_space, VMEM),
        scratch_shapes=[
            pltpu.VMEM((2, 4096, 128), jnp.float32),
            pltpu.VMEM((2, 2, 3, DEVICES, 128), jnp.float32),
            pltpu.VMEM((DEVICES, 128), jnp.int32),
            pltpu.SMEM((DEVICES, 128), jnp.int32),
            pltpu.SemaphoreType.DMA((8,)),
            pltpu.SemaphoreType.DMA,
        ],
        compiler_params=pltpu.CompilerParams(vmem_limit_bytes=40 << 20),
        name="second_pass",
    )(got, long_both, turn_second, short_second)
    back = exchange(answer.reshape(DEVICES, 1, 128)).reshape(DEVICES, 128)
    samples = pl.pallas_call(
        last_kernel,
        out_shape=jax.ShapeDtypeStruct((2, DEVICES), jnp.float32),
        in_specs=[VMEM] * 3,
        out_specs=VMEM,
        name="samples",
    )(back, block, site_cell)
    field = field.reshape(2, 8, 64, 8, 128).transpose(0, 1, 3, 2, 4).reshape(2, ROWS, GRID)
    return field, samples


def solution(mesh):
    return jax.shard_map(
        per_device,
        mesh=mesh,
        in_specs=(
            P(None, AXES, None),
            P(AXES, None),
            P(AXES),
            P(None, AXES),
            P(None, AXES),
        ),
        out_specs=(P(None, AXES, None), P(None, AXES)),
        check_vma=False,
    )
```

```python
import numpy as np
import ml_dtypes
import jax
import jax.numpy as jnp
from jax import lax
from jax.experimental import pallas as pl
from jax.experimental.pallas import tpu as pltpu
from jax.sharding import PartitionSpec as P

GRID = 8192
DEVICES = 128
ROWS = 64
MESSAGE = 65
PITCH = 72
CHUNKS = ((0, 2), (2, 3), (5, 3))
AXES = ("row", "col")
VMEM = pl.BlockSpec(memory_space=pltpu.VMEM)
HIGH = lax.Precision.HIGHEST
LAST = (((1,), (1,)), ((), ()))


def phase(product, length):
    angle = 2.0 * np.pi / length * (product % length)
    return np.cos(angle), np.sin(angle)


def complex_matrix(cosine, sine):
    return np.block([[cosine, -sine], [sine, cosine]])


def split_table(table):
    high = table.astype(ml_dtypes.bfloat16)
    low = (table - high.astype(np.float64)).astype(ml_dtypes.bfloat16)
    return high, low


def make_tables():
    short, long = np.arange(64), np.arange(128)
    high, low = split_table(complex_matrix(*phase(np.outer(short, short), 64)))
    short_first = np.block([[high, high], [low, np.zeros_like(low)]])
    turn_first = np.stack(phase(np.outer(short, long), GRID)).astype(np.float32)
    long_both = np.stack(split_table(complex_matrix(*phase(np.outer(long, long), 128))))
    turn_second = np.stack(phase(np.outer(long, short), GRID)) / GRID
    turn_second = np.concatenate([turn_second, turn_second], axis=2).astype(np.float32)
    cosine, sine = phase(np.outer(short, short), 64)
    pair = np.eye(2)
    short_second = np.stack(
        split_table(complex_matrix(np.kron(pair, cosine), np.kron(pair, sine)))
    )
    return short_first, turn_first, long_both, turn_second, short_second


def split(value):
    high = value.astype(jnp.bfloat16)
    low = (value - high.astype(jnp.float32)).astype(jnp.bfloat16)
    return high, low


def dot(left, right, dims=(((1,), (0,)), ((), ()))):
    return lax.dot_general(left, right, dims, preferred_element_type=jnp.float32)


def split_dot(table, value, dims=(((1,), (0,)), ((), ()))):
    high, low = split(value)
    return dot(table[0], high, dims) + dot(table[0], low, dims) + dot(table[1], high, dims)


def site_slots(block):
    wide = jnp.broadcast_to(block.astype(jnp.float32), (DEVICES, DEVICES))
    before = lax.broadcasted_iota(jnp.int32, (DEVICES, DEVICES), 0)
    after = lax.broadcasted_iota(jnp.int32, (DEVICES, DEVICES), 1)
    earlier = (wide == wide.T) & (before < after)
    return jnp.sum(jnp.where(earlier, 1.0, 0.0), axis=0, keepdims=True)


def site_requests(block, cell, frac):
    slot = site_slots(block)
    row, column = cell[0:1], cell[1:2]
    column_next = (column + 1) & (GRID - 1)
    part_row, part_col = frac[0:1], frac[1:2]
    edge = row == ROWS - 1
    tile = (column >> 7).astype(jnp.float32)
    tile_next = (column_next >> 7).astype(jnp.float32)
    line = row.astype(jnp.float32)
    lane = (column & 127).astype(jnp.float32)
    lane_next = (column_next & 127).astype(jnp.float32)
    lower = jnp.where(edge, 0.0, part_row)
    own = [
        PITCH * tile + line,
        PITCH * tile_next + line,
        lane,
        lane_next,
        (1 - part_row) * (1 - part_col),
        (1 - part_row) * part_col,
        lower * (1 - part_col),
        lower * part_col,
    ]
    halo = [
        tile,
        tile_next,
        lane,
        lane_next,
        part_row * (1 - part_col),
        part_row * part_col,
    ]
    blank = jnp.zeros((1, DEVICES), jnp.float32)
    groups = []
    for at, values in ((0, own), (8, own), (16, halo), (22, halo)):
        lines = [blank] * at + values
        groups.append(jnp.concatenate(lines + [blank] * (DEVICES - len(lines)), axis=0))
    owner = lax.broadcasted_iota(jnp.int32, (DEVICES, DEVICES), 0)
    here = owner == block
    below = (owner == ((block + 1) & (DEVICES - 1))) & edge
    picks = []
    for mask in (here, below):
        for which in (0.0, 1.0):
            picks.append(jnp.where(mask & (slot == which), 1.0, 0.0))
    return lax.dot_general(
        jnp.concatenate(picks, axis=1),
        jnp.concatenate(groups, axis=1),
        LAST,
        precision=HIGH,
        preferred_element_type=jnp.float32,
    )


def first_kernel(
    noise_hbm,
    power_hbm,
    block_hbm,
    cell_hbm,
    frac_hbm,
    short_hbm,
    turn_hbm,
    long_hbm,
    out_ref,
    noise,
    power,
    block_ref,
    cell_ref,
    frac_ref,
    short_ref,
    turn_ref,
    long_ref,
    middle,
    noise_sem,
    power_sem,
    small_sem,
):
    small = [
        pltpu.make_async_copy(source, target, small_sem.at[k])
        for k, (source, target) in enumerate(
            (
                (block_hbm, block_ref),
                (cell_hbm, cell_ref),
                (frac_hbm, frac_ref),
                (short_hbm, short_ref),
                (turn_hbm, turn_ref),
                (long_hbm, long_ref),
            )
        )
    ]
    large = []
    for k, (start, count) in enumerate(CHUNKS):
        span = pl.ds(start, count)
        large.append(
            (
                pltpu.make_async_copy(power_hbm.at[span], power.at[span], power_sem.at[k]),
                pltpu.make_async_copy(noise_hbm.at[:, span], noise.at[:, span], noise_sem.at[k]),
            )
        )
    for copy in small[:5] + list(large[0]) + small[5:]:
        copy.start()
    for pair in large[1:]:
        pair[0].start()
        pair[1].start()
    for copy in small[:3]:
        copy.wait()
    out_ref[pl.ds(MESSAGE - 1, DEVICES, stride=MESSAGE), :] = site_requests(
        block_ref[...], cell_ref[...], frac_ref[...]
    )
    small[3].wait()
    small[4].wait()
    for k, (start, count) in enumerate(CHUNKS):
        large[k][0].wait()
        large[k][1].wait()
        for first in range(8 * start, 8 * (start + count), 2):
            parts = []
            for row in (first, first + 1):
                at = pl.ds(row % 8, 64, stride=8)
                level = power[row // 8, at, :]
                amplitude = level * lax.rsqrt(level)
                stacked = jnp.concatenate(
                    [amplitude * noise[0, row // 8, at, :], amplitude * noise[1, row // 8, at, :]],
                    axis=0,
                )
                parts.append(jnp.concatenate(split(stacked), axis=0))
            sums = dot(short_ref[...], jnp.concatenate(parts, axis=1))
            sums = sums[:128] + sums[128:]
            for k2 in range(2):
                real = sums[:64, 128 * k2 : 128 * k2 + 128]
                imag = sums[64:, 128 * k2 : 128 * k2 + 128]
                at = pl.ds(first + k2, 64, stride=PITCH)
                middle[0, at, :] = real * turn_ref[0] - imag * turn_ref[1]
                middle[1, at, :] = real * turn_ref[1] + imag * turn_ref[0]
    small[5].wait()
    for step in range(16):
        value = jnp.concatenate(
            [
                jnp.concatenate(
                    [middle[part, pl.ds(PITCH * (4 * step + k), 64), :] for k in range(4)], axis=0
                )
                for part in range(2)
            ],
            axis=1,
        )
        sums = split_dot(long_ref, value, LAST)
        for part in range(2):
            for k in range(2):
                j = 32 * part + 2 * step + k
                out_ref[pl.ds(j, DEVICES, stride=MESSAGE), :] = sums[
                    128 * part : 128 * part + 128, 128 * k : 128 * k + 128
                ]


def second_kernel(
    got_ref,
    long_ref,
    turn_ref,
    short_ref,
    field_hbm,
    answer_ref,
    tiles,
    field,
    picked,
    code_vmem,
    code_smem,
    field_sem,
    code_sem,
):
    for part in range(2):
        field[part, pl.ds(ROWS, 64, stride=PITCH), :] = jnp.zeros((64, 128), jnp.float32)
    asked = got_ref[pl.ds(MESSAGE - 1, DEVICES, stride=MESSAGE), :]
    code_vmem[...] = (asked + 0.5).astype(jnp.int32)
    code_copy = pltpu.make_async_copy(code_vmem, code_smem, code_sem)
    code_copy.start()
    copies = []
    for i in range(8):
        for half in range(2):
            pair = 4 * i + 2 * half
            value = jnp.concatenate(
                [
                    jnp.concatenate(
                        [
                            got_ref[pl.ds(32 * part + pair + k, DEVICES, stride=MESSAGE), :]
                            for k in range(2)
                        ],
                        axis=1,
                    )
                    for part in range(2)
                ],
                axis=0,
            )
            sums = split_dot(long_ref, value)
            turned = []
            for k in range(2):
                real = sums[:128, 128 * k : 128 * k + 128]
                imag = sums[128:, 128 * k : 128 * k + 128]
                turned.append(
                    jnp.concatenate(
                        [
                            real * turn_ref[0] - imag * turn_ref[1],
                            real * turn_ref[1] + imag * turn_ref[0],
                        ],
                        axis=1,
                    )
                )
            sums = split_dot(short_ref, jnp.concatenate(turned, axis=0), LAST)
            for part in range(2):
                for odd in range(2):
                    for k in range(2):
                        top = 128 * part + 64 * odd
                        row = 4 * half + 2 * k + odd
                        value = sums[top : top + 64, 128 * k : 128 * k + 128]
                        tiles[part, pl.ds(512 * i + row, 64, stride=8), :] = value
                        field[part, pl.ds(8 * i + row, 64, stride=PITCH), :] = value
        copies.append(
            pltpu.make_async_copy(
                tiles.at[:, pl.ds(512 * i, 512)], field_hbm.at[:, i], field_sem.at[i]
            )
        )
        copies[-1].start()
    code_copy.wait()

    head = lax.broadcasted_iota(jnp.int32, (2, 128), 1) == 0

    def gather(device, carry):
        for which in range(2):
            line = code_smem[device, 8 * which]
            line_next = code_smem[device, 8 * which + 1]
            for part in range(2):
                picked[which, part, pl.ds(2 * device, 2), :] = jnp.where(
                    head,
                    field[part, pl.ds(line_next, 2), :],
                    field[part, pl.ds(line, 2), :],
                )
        return carry

    lax.fori_loop(0, DEVICES, gather, 0, unroll=8)
    lanes = lax.broadcasted_iota(jnp.int32, (DEVICES, 128), 1).astype(jnp.float32)
    answer = jnp.zeros((DEVICES, 128), jnp.float32)

    def column(at):
        return asked[:, at : at + 1]

    first_row = pl.ds(0, 64, stride=PITCH)
    terms = split(jnp.concatenate([field[0, first_row, :], field[1, first_row, :]], axis=1))
    places = lax.broadcasted_iota(jnp.int32, (DEVICES, 128), 1) & 63
    places = places.astype(jnp.float32)
    masks = [
        jnp.where(places == column(16 + 6 * which + k), 1.0, 0.0).astype(jnp.bfloat16)
        for k in range(2)
        for which in range(2)
    ]
    beyond = dot(jnp.concatenate(masks, axis=0), jnp.concatenate(terms, axis=0))
    for which in range(2):
        own, halo = 8 * which, 16 + 6 * which

        def weight(lane, value):
            return jnp.where(lanes == column(lane), column(value), 0.0)

        upper = weight(own + 2, own + 4) + weight(own + 3, own + 5)
        lower = weight(own + 2, own + 6) + weight(own + 3, own + 7)
        edge, edge_next = weight(halo + 2, halo + 4), weight(halo + 3, halo + 5)
        for part in range(2):
            value = upper * picked[which, part, pl.ds(0, DEVICES, stride=2), :]
            value += lower * picked[which, part, pl.ds(1, DEVICES, stride=2), :]
            answer = jnp.where(
                lanes == 2 * which + part, jnp.sum(value, axis=1, keepdims=True), answer
            )
            span = slice(128 * part, 128 * part + 128)
            value = edge * beyond[128 * which : 128 * which + 128, span]
            value += edge_next * beyond[256 + 128 * which : 384 + 128 * which, span]
            answer = jnp.where(
                lanes == 4 + 2 * which + part, jnp.sum(value, axis=1, keepdims=True), answer
            )
    answer_ref[...] = answer
    for copy in copies:
        copy.wait()


def last_kernel(answer_ref, block_ref, cell_ref, out_ref):
    block = block_ref[...]
    slot = site_slots(block)
    edge = cell_ref[0:1] == ROWS - 1
    owner = lax.broadcasted_iota(jnp.int32, (DEVICES, DEVICES), 0)
    values = answer_ref[...].T[:8]
    masks = jnp.concatenate([owner == block, owner == ((block + 1) & (DEVICES - 1))], axis=1)
    high, middle = split(values)
    rest = values - high.astype(jnp.float32) - middle.astype(jnp.float32)
    terms = jnp.concatenate([high, middle, rest.astype(jnp.bfloat16)], axis=0)
    sums = dot(terms, jnp.where(masks, 1.0, 0.0).astype(jnp.bfloat16))
    sums = sums[0:8] + sums[8:16] + sums[16:24]
    here, below = sums[:, :DEVICES], sums[:, DEVICES:]
    own = jnp.where(slot == 0.0, here[0:2], here[2:4])
    halo = jnp.where(slot == 0.0, below[4:6], below[6:8])
    out_ref[...] = own + jnp.where(edge, halo, 0.0)


def exchange(value):
    return lax.all_to_all(value, AXES, split_axis=0, concat_axis=0, tiled=True)


def per_device(spectrum_noise, power_spectrum, site_block, site_cell, site_frac):
    short_first, turn_first, long_both, turn_second, short_second = make_tables()
    any_space = pl.BlockSpec(memory_space=pl.ANY)
    noise = spectrum_noise.reshape(2, 8, 8, 64, 128).transpose(0, 1, 3, 2, 4).reshape(2, 8, 512, 128)
    power = power_spectrum.reshape(8, 8, 64, 128).transpose(0, 2, 1, 3).reshape(8, 512, 128)
    block = site_block.reshape(1, DEVICES)
    operands = [
        pltpu.with_memory_space_constraint(operand, pltpu.HBM)
        for operand in map(
            jnp.asarray,
            (noise, power, block, site_cell, site_frac, short_first, turn_first, long_both),
        )
    ]
    sent = pl.pallas_call(
        first_kernel,
        out_shape=jax.ShapeDtypeStruct((DEVICES * MESSAGE, 128), jnp.float32),
        in_specs=[pl.BlockSpec(memory_space=pltpu.HBM)] * 8,
        out_specs=VMEM,
        scratch_shapes=[
            pltpu.VMEM((2, 8, 512, 128), jnp.float32),
            pltpu.VMEM((8, 512, 128), jnp.float32),
            pltpu.VMEM((1, DEVICES), jnp.int32),
            pltpu.VMEM((2, DEVICES), jnp.int32),
            pltpu.VMEM((2, DEVICES), jnp.float32),
            pltpu.VMEM((256, 256), jnp.bfloat16),
            pltpu.VMEM((2, 64, 128), jnp.float32),
            pltpu.VMEM((2, 256, 256), jnp.bfloat16),
            pltpu.VMEM((2, 64 * PITCH, 128), jnp.float32),
            pltpu.SemaphoreType.DMA((len(CHUNKS),)),
            pltpu.SemaphoreType.DMA((len(CHUNKS),)),
            pltpu.SemaphoreType.DMA((6,)),
        ],
        compiler_params=pltpu.CompilerParams(vmem_limit_bytes=40 << 20),
        name="first_pass",
    )(*operands)
    got = exchange(sent.reshape(DEVICES * MESSAGE, 1, 128)).reshape(DEVICES * MESSAGE, 128)
    field, answer = pl.pallas_call(
        second_kernel,
        out_shape=(
            jax.ShapeDtypeStruct((2, 8, 512, 128), jnp.float32),
            jax.ShapeDtypeStruct((DEVICES, 128), jnp.float32),
        ),
        in_specs=[VMEM] * 4,
        out_specs=(any_space, VMEM),
        scratch_shapes=[
            pltpu.VMEM((2, 4096, 128), jnp.float32),
            pltpu.VMEM((2, 64 * PITCH, 128), jnp.float32),
            pltpu.VMEM((2, 2, 2 * DEVICES, 128), jnp.float32),
            pltpu.VMEM((DEVICES, 128), jnp.int32),
            pltpu.SMEM((DEVICES, 128), jnp.int32),
            pltpu.SemaphoreType.DMA((8,)),
            pltpu.SemaphoreType.DMA,
        ],
        compiler_params=pltpu.CompilerParams(vmem_limit_bytes=40 << 20),
        name="second_pass",
    )(got, long_both, turn_second, short_second)
    back = exchange(answer.reshape(DEVICES, 1, 128)).reshape(DEVICES, 128)
    samples = pl.pallas_call(
        last_kernel,
        out_shape=jax.ShapeDtypeStruct((2, DEVICES), jnp.float32),
        in_specs=[VMEM] * 3,
        out_specs=VMEM,
        name="samples",
    )(back, block, site_cell)
    field = field.reshape(2, 8, 64, 8, 128).transpose(0, 1, 3, 2, 4).reshape(2, ROWS, GRID)
    return field, samples


def solution(mesh):
    return jax.shard_map(
        per_device,
        mesh=mesh,
        in_specs=(
            P(None, AXES, None),
            P(AXES, None),
            P(AXES),
            P(None, AXES),
            P(None, AXES),
        ),
        out_specs=(P(None, AXES, None), P(None, AXES)),
        check_vma=False,
    )
```

```python
import numpy as np
import ml_dtypes
import jax
import jax.numpy as jnp
from jax import lax
from jax.experimental import pallas as pl
from jax.experimental.pallas import tpu as pltpu
from jax.sharding import PartitionSpec as P

GRID = 8192
DEVICES = 128
ROWS = 64
MESSAGE = 65
PITCH = 72
CHUNKS = ((0, 2), (2, 3), (5, 3))
AXES = ("row", "col")
VMEM = pl.BlockSpec(memory_space=pltpu.VMEM)
HIGH = lax.Precision.HIGHEST
LAST = (((1,), (1,)), ((), ()))


def phase(product, length):
    angle = 2.0 * np.pi / length * (product % length)
    return np.cos(angle), np.sin(angle)


def complex_matrix(cosine, sine):
    return np.block([[cosine, -sine], [sine, cosine]])


def split_table(table):
    high = table.astype(ml_dtypes.bfloat16)
    low = (table - high.astype(np.float64)).astype(ml_dtypes.bfloat16)
    return high, low


def make_tables():
    short, long = np.arange(64), np.arange(128)
    high, low = split_table(complex_matrix(*phase(np.outer(short, short), 64)))
    short_first = np.block([[high, high], [low, np.zeros_like(low)]])
    turn_first = np.stack(phase(np.outer(short, long), GRID)).astype(np.float32)
    long_both = np.stack(split_table(complex_matrix(*phase(np.outer(long, long), 128))))
    turn_second = np.stack(phase(np.outer(long, short), GRID)) / GRID
    turn_second = np.concatenate([turn_second, turn_second], axis=2).astype(np.float32)
    cosine, sine = phase(np.outer(short, short), 64)
    pair = np.eye(2)
    short_second = np.stack(
        split_table(complex_matrix(np.kron(pair, cosine), np.kron(pair, sine)))
    )
    return short_first, turn_first, long_both, turn_second, short_second


def split(value):
    high = value.astype(jnp.bfloat16)
    low = (value - high.astype(jnp.float32)).astype(jnp.bfloat16)
    return high, low


def dot(left, right, dims=(((1,), (0,)), ((), ()))):
    return lax.dot_general(left, right, dims, preferred_element_type=jnp.float32)


def split_dot(table, value, dims=(((1,), (0,)), ((), ()))):
    high, low = split(value)
    return dot(table[0], low, dims) + dot(table[1], high, dims) + dot(table[0], high, dims)


def site_slots(block):
    wide = jnp.broadcast_to(block.astype(jnp.float32), (DEVICES, DEVICES))
    before = lax.broadcasted_iota(jnp.int32, (DEVICES, DEVICES), 0)
    after = lax.broadcasted_iota(jnp.int32, (DEVICES, DEVICES), 1)
    earlier = (wide == wide.T) & (before < after)
    return jnp.sum(jnp.where(earlier, 1.0, 0.0), axis=0, keepdims=True)


def site_requests(block, cell, frac):
    slot = site_slots(block)
    row, column = cell[0:1], cell[1:2]
    column_next = (column + 1) & (GRID - 1)
    part_row, part_col = frac[0:1], frac[1:2]
    edge = row == ROWS - 1
    tile = (column >> 7).astype(jnp.float32)
    tile_next = (column_next >> 7).astype(jnp.float32)
    line = row.astype(jnp.float32)
    lane = (column & 127).astype(jnp.float32)
    lane_next = (column_next & 127).astype(jnp.float32)
    lower = jnp.where(edge, 0.0, part_row)
    own = [
        PITCH * tile + line,
        PITCH * tile_next + line,
        lane,
        lane_next,
        (1 - part_row) * (1 - part_col),
        (1 - part_row) * part_col,
        lower * (1 - part_col),
        lower * part_col,
    ]
    halo = [
        tile,
        tile_next,
        lane,
        lane_next,
        part_row * (1 - part_col),
        part_row * part_col,
    ]
    blank = jnp.zeros((1, DEVICES), jnp.float32)
    groups = []
    for at, values in ((0, own), (8, own), (16, halo), (22, halo)):
        lines = [blank] * at + values
        groups.append(jnp.concatenate(lines + [blank] * (DEVICES - len(lines)), axis=0))
    owner = lax.broadcasted_iota(jnp.int32, (DEVICES, DEVICES), 0)
    here = owner == block
    below = (owner == ((block + 1) & (DEVICES - 1))) & edge
    picks = []
    for mask in (here, below):
        for which in (0.0, 1.0):
            picks.append(jnp.where(mask & (slot == which), 1.0, 0.0))
    return lax.dot_general(
        jnp.concatenate(picks, axis=1),
        jnp.concatenate(groups, axis=1),
        LAST,
        precision=HIGH,
        preferred_element_type=jnp.float32,
    )


def first_kernel(
    noise_hbm,
    power_hbm,
    block_hbm,
    cell_hbm,
    frac_hbm,
    short_hbm,
    turn_hbm,
    long_hbm,
    out_ref,
    noise,
    power,
    block_ref,
    cell_ref,
    frac_ref,
    short_ref,
    turn_ref,
    long_ref,
    middle,
    noise_sem,
    power_sem,
    small_sem,
):
    small = [
        pltpu.make_async_copy(source, target, small_sem.at[k])
        for k, (source, target) in enumerate(
            (
                (block_hbm, block_ref),
                (cell_hbm, cell_ref),
                (frac_hbm, frac_ref),
                (short_hbm, short_ref),
                (turn_hbm, turn_ref),
                (long_hbm, long_ref),
            )
        )
    ]
    large = []
    for k, (start, count) in enumerate(CHUNKS):
        span = pl.ds(start, count)
        large.append(
            (
                pltpu.make_async_copy(power_hbm.at[span], power.at[span], power_sem.at[k]),
                pltpu.make_async_copy(noise_hbm.at[:, span], noise.at[:, span], noise_sem.at[k]),
            )
        )
    for copy in small[:5] + list(large[0]) + small[5:]:
        copy.start()
    for pair in large[1:]:
        pair[0].start()
        pair[1].start()
    for copy in small[:3]:
        copy.wait()
    out_ref[pl.ds(MESSAGE - 1, DEVICES, stride=MESSAGE), :] = site_requests(
        block_ref[...], cell_ref[...], frac_ref[...]
    )
    small[3].wait()
    small[4].wait()
    for k, (start, count) in enumerate(CHUNKS):
        large[k][0].wait()
        large[k][1].wait()
        for first in range(8 * start, 8 * (start + count), 2):
            parts = []
            for row in (first, first + 1):
                at = pl.ds(row % 8, 64, stride=8)
                level = power[row // 8, at, :]
                amplitude = level * lax.rsqrt(level)
                stacked = jnp.concatenate(
                    [amplitude * noise[0, row // 8, at, :], amplitude * noise[1, row // 8, at, :]],
                    axis=0,
                )
                parts.append(jnp.concatenate(split(stacked), axis=0))
            sums = dot(short_ref[...], jnp.concatenate(parts, axis=1))
            sums = sums[:128] + sums[128:]
            for k2 in range(2):
                real = sums[:64, 128 * k2 : 128 * k2 + 128]
                imag = sums[64:, 128 * k2 : 128 * k2 + 128]
                at = pl.ds(first + k2, 64, stride=PITCH)
                middle[0, at, :] = real * turn_ref[0] - imag * turn_ref[1]
                middle[1, at, :] = real * turn_ref[1] + imag * turn_ref[0]
    small[5].wait()
    for step in range(16):
        value = jnp.concatenate(
            [
                jnp.concatenate(
                    [middle[part, pl.ds(PITCH * (4 * step + k), 64), :] for k in range(4)], axis=0
                )
                for part in range(2)
            ],
            axis=1,
        )
        sums = split_dot(long_ref, value, LAST)
        for part in range(2):
            for k in range(2):
                j = 32 * part + 2 * step + k
                out_ref[pl.ds(j, DEVICES, stride=MESSAGE), :] = sums[
                    128 * part : 128 * part + 128, 128 * k : 128 * k + 128
                ]


def second_kernel(
    got_ref,
    long_ref,
    turn_ref,
    short_ref,
    field_hbm,
    answer_ref,
    tiles,
    field,
    picked,
    code_vmem,
    code_smem,
    field_sem,
    code_sem,
):
    for part in range(2):
        field[part, pl.ds(ROWS, 64, stride=PITCH), :] = jnp.zeros((64, 128), jnp.float32)
    asked = got_ref[pl.ds(MESSAGE - 1, DEVICES, stride=MESSAGE), :]
    code_vmem[...] = (asked + 0.5).astype(jnp.int32)
    code_copy = pltpu.make_async_copy(code_vmem, code_smem, code_sem)
    code_copy.start()
    copies = []
    for i in range(8):
        for half in range(2):
            pair = 4 * i + 2 * half
            value = jnp.concatenate(
                [
                    jnp.concatenate(
                        [
                            got_ref[pl.ds(32 * part + pair + k, DEVICES, stride=MESSAGE), :]
                            for k in range(2)
                        ],
                        axis=1,
                    )
                    for part in range(2)
                ],
                axis=0,
            )
            sums = split_dot(long_ref, value)
            turned = []
            for k in range(2):
                real = sums[:128, 128 * k : 128 * k + 128]
                imag = sums[128:, 128 * k : 128 * k + 128]
                turned.append(
                    jnp.concatenate(
                        [
                            real * turn_ref[0] - imag * turn_ref[1],
                            real * turn_ref[1] + imag * turn_ref[0],
                        ],
                        axis=1,
                    )
                )
            sums = split_dot(short_ref, jnp.concatenate(turned, axis=0), LAST)
            for part in range(2):
                for odd in range(2):
                    for k in range(2):
                        top = 128 * part + 64 * odd
                        row = 4 * half + 2 * k + odd
                        value = sums[top : top + 64, 128 * k : 128 * k + 128]
                        tiles[part, pl.ds(512 * i + row, 64, stride=8), :] = value
                        field[part, pl.ds(8 * i + row, 64, stride=PITCH), :] = value
        copies.append(
            pltpu.make_async_copy(
                tiles.at[:, pl.ds(512 * i, 512)], field_hbm.at[:, i], field_sem.at[i]
            )
        )
        copies[-1].start()
    code_copy.wait()

    head = lax.broadcasted_iota(jnp.int32, (2, 128), 1) == 0

    def gather(device, carry):
        for which in range(2):
            line = code_smem[device, 8 * which]
            line_next = code_smem[device, 8 * which + 1]
            for part in range(2):
                picked[which, part, pl.ds(2 * device, 2), :] = jnp.where(
                    head,
                    field[part, pl.ds(line_next, 2), :],
                    field[part, pl.ds(line, 2), :],
                )
        return carry

    lax.fori_loop(0, DEVICES, gather, 0, unroll=8)
    lanes = lax.broadcasted_iota(jnp.int32, (DEVICES, 128), 1).astype(jnp.float32)
    answer = jnp.zeros((DEVICES, 128), jnp.float32)

    def column(at):
        return asked[:, at : at + 1]

    first_row = pl.ds(0, 64, stride=PITCH)
    terms = split(jnp.concatenate([field[0, first_row, :], field[1, first_row, :]], axis=1))
    places = lax.broadcasted_iota(jnp.int32, (DEVICES, 128), 1) & 63
    places = places.astype(jnp.float32)
    masks = [
        jnp.where(places == column(16 + 6 * which + k), 1.0, 0.0).astype(jnp.bfloat16)
        for k in range(2)
        for which in range(2)
    ]
    beyond = dot(jnp.concatenate(masks, axis=0), jnp.concatenate(terms, axis=0))
    for which in range(2):
        own, halo = 8 * which, 16 + 6 * which

        def weight(lane, value):
            return jnp.where(lanes == column(lane), column(value), 0.0)

        upper = weight(own + 2, own + 4) + weight(own + 3, own + 5)
        lower = weight(own + 2, own + 6) + weight(own + 3, own + 7)
        edge, edge_next = weight(halo + 2, halo + 4), weight(halo + 3, halo + 5)
        for part in range(2):
            value = upper * picked[which, part, pl.ds(0, DEVICES, stride=2), :]
            value += lower * picked[which, part, pl.ds(1, DEVICES, stride=2), :]
            answer = jnp.where(
                lanes == 2 * which + part, jnp.sum(value, axis=1, keepdims=True), answer
            )
            span = slice(128 * part, 128 * part + 128)
            value = edge * beyond[128 * which : 128 * which + 128, span]
            value += edge_next * beyond[256 + 128 * which : 384 + 128 * which, span]
            answer = jnp.where(
                lanes == 4 + 2 * which + part, jnp.sum(value, axis=1, keepdims=True), answer
            )
    answer_ref[...] = answer
    for copy in copies:
        copy.wait()


def last_kernel(answer_ref, block_ref, cell_ref, out_ref):
    block = block_ref[...]
    slot = site_slots(block)
    edge = cell_ref[0:1] == ROWS - 1
    owner = lax.broadcasted_iota(jnp.int32, (DEVICES, DEVICES), 0)
    values = answer_ref[...].T[:8]
    masks = jnp.concatenate([owner == block, owner == ((block + 1) & (DEVICES - 1))], axis=1)
    high, middle = split(values)
    rest = values - high.astype(jnp.float32) - middle.astype(jnp.float32)
    terms = jnp.concatenate([high, middle, rest.astype(jnp.bfloat16)], axis=0)
    sums = dot(terms, jnp.where(masks, 1.0, 0.0).astype(jnp.bfloat16))
    sums = sums[0:8] + sums[8:16] + sums[16:24]
    here, below = sums[:, :DEVICES], sums[:, DEVICES:]
    own = jnp.where(slot == 0.0, here[0:2], here[2:4])
    halo = jnp.where(slot == 0.0, below[4:6], below[6:8])
    out_ref[...] = own + jnp.where(edge, halo, 0.0)


def exchange(value):
    return lax.all_to_all(value, AXES, split_axis=0, concat_axis=0, tiled=True)


def per_device(spectrum_noise, power_spectrum, site_block, site_cell, site_frac):
    short_first, turn_first, long_both, turn_second, short_second = make_tables()
    any_space = pl.BlockSpec(memory_space=pl.ANY)
    noise = spectrum_noise.reshape(2, 8, 8, 64, 128).transpose(0, 1, 3, 2, 4).reshape(2, 8, 512, 128)
    power = power_spectrum.reshape(8, 8, 64, 128).transpose(0, 2, 1, 3).reshape(8, 512, 128)
    block = site_block.reshape(1, DEVICES)
    operands = [
        pltpu.with_memory_space_constraint(operand, pltpu.HBM)
        for operand in map(
            jnp.asarray,
            (noise, power, block, site_cell, site_frac, short_first, turn_first, long_both),
        )
    ]
    sent = pl.pallas_call(
        first_kernel,
        out_shape=jax.ShapeDtypeStruct((DEVICES * MESSAGE, 128), jnp.float32),
        in_specs=[pl.BlockSpec(memory_space=pltpu.HBM)] * 8,
        out_specs=VMEM,
        scratch_shapes=[
            pltpu.VMEM((2, 8, 512, 128), jnp.float32),
            pltpu.VMEM((8, 512, 128), jnp.float32),
            pltpu.VMEM((1, DEVICES), jnp.int32),
            pltpu.VMEM((2, DEVICES), jnp.int32),
            pltpu.VMEM((2, DEVICES), jnp.float32),
            pltpu.VMEM((256, 256), jnp.bfloat16),
            pltpu.VMEM((2, 64, 128), jnp.float32),
            pltpu.VMEM((2, 256, 256), jnp.bfloat16),
            pltpu.VMEM((2, 64 * PITCH, 128), jnp.float32),
            pltpu.SemaphoreType.DMA((len(CHUNKS),)),
            pltpu.SemaphoreType.DMA((len(CHUNKS),)),
            pltpu.SemaphoreType.DMA((6,)),
        ],
        compiler_params=pltpu.CompilerParams(vmem_limit_bytes=40 << 20),
        name="first_pass",
    )(*operands)
    got = exchange(sent.reshape(DEVICES * MESSAGE, 1, 128)).reshape(DEVICES * MESSAGE, 128)
    field, answer = pl.pallas_call(
        second_kernel,
        out_shape=(
            jax.ShapeDtypeStruct((2, 8, 512, 128), jnp.float32),
            jax.ShapeDtypeStruct((DEVICES, 128), jnp.float32),
        ),
        in_specs=[VMEM] * 4,
        out_specs=(any_space, VMEM),
        scratch_shapes=[
            pltpu.VMEM((2, 4096, 128), jnp.float32),
            pltpu.VMEM((2, 64 * PITCH, 128), jnp.float32),
            pltpu.VMEM((2, 2, 2 * DEVICES, 128), jnp.float32),
            pltpu.VMEM((DEVICES, 128), jnp.int32),
            pltpu.SMEM((DEVICES, 128), jnp.int32),
            pltpu.SemaphoreType.DMA((8,)),
            pltpu.SemaphoreType.DMA,
        ],
        compiler_params=pltpu.CompilerParams(vmem_limit_bytes=40 << 20),
        name="second_pass",
    )(got, long_both, turn_second, short_second)
    back = exchange(answer.reshape(DEVICES, 1, 128)).reshape(DEVICES, 128)
    samples = pl.pallas_call(
        last_kernel,
        out_shape=jax.ShapeDtypeStruct((2, DEVICES), jnp.float32),
        in_specs=[VMEM] * 3,
        out_specs=VMEM,
        name="samples",
    )(back, block, site_cell)
    field = field.reshape(2, 8, 64, 8, 128).transpose(0, 1, 3, 2, 4).reshape(2, ROWS, GRID)
    return field, samples


def solution(mesh):
    return jax.shard_map(
        per_device,
        mesh=mesh,
        in_specs=(
            P(None, AXES, None),
            P(AXES, None),
            P(AXES),
            P(None, AXES),
            P(None, AXES),
        ),
        out_specs=(P(None, AXES, None), P(None, AXES)),
        check_vma=False,
    )
```

```python
import numpy as np
import ml_dtypes
import jax
import jax.numpy as jnp
from jax import lax
from jax.experimental import pallas as pl
from jax.experimental.pallas import tpu as pltpu
from jax.sharding import PartitionSpec as P

GRID = 8192
DEVICES = 128
ROWS = 64
MESSAGE = 65
PITCH = 72
CHUNKS = ((0, 2), (2, 3), (5, 3))
AXES = ("row", "col")
VMEM = pl.BlockSpec(memory_space=pltpu.VMEM)
HIGH = lax.Precision.HIGHEST
LAST = (((1,), (1,)), ((), ()))


def phase(product, length):
    angle = 2.0 * np.pi / length * (product % length)
    return np.cos(angle), np.sin(angle)


def complex_matrix(cosine, sine):
    return np.block([[cosine, -sine], [sine, cosine]])


def split_table(table):
    high = table.astype(ml_dtypes.bfloat16)
    low = (table - high.astype(np.float64)).astype(ml_dtypes.bfloat16)
    return high, low


def make_tables():
    short, long = np.arange(64), np.arange(128)
    high, low = split_table(complex_matrix(*phase(np.outer(short, short), 64)))
    short_first = np.block([[high, high], [low, np.zeros_like(low)]])
    turn_first = np.stack(phase(np.outer(short, long), GRID)).astype(np.float32)
    long_both = np.stack(split_table(complex_matrix(*phase(np.outer(long, long), 128))))
    turn_second = np.stack(phase(np.outer(long, short), GRID)) / GRID
    turn_second = np.concatenate([turn_second, turn_second], axis=2).astype(np.float32)
    cosine, sine = phase(np.outer(short, short), 64)
    pair = np.eye(2)
    short_second = np.stack(
        split_table(complex_matrix(np.kron(pair, cosine), np.kron(pair, sine)))
    )
    return short_first, turn_first, long_both, turn_second, short_second


def split(value):
    high = value.astype(jnp.bfloat16)
    low = (value - high.astype(jnp.float32)).astype(jnp.bfloat16)
    return high, low


def dot(left, right, dims=(((1,), (0,)), ((), ()))):
    return lax.dot_general(left, right, dims, preferred_element_type=jnp.float32)


def split_dot(table, value, dims=(((1,), (0,)), ((), ()))):
    high, low = split(value)
    return dot(table[0], low, dims) + dot(table[1], high, dims) + dot(table[0], high, dims)


def site_slots(block):
    wide = jnp.broadcast_to(block.astype(jnp.float32), (DEVICES, DEVICES))
    before = lax.broadcasted_iota(jnp.int32, (DEVICES, DEVICES), 0)
    after = lax.broadcasted_iota(jnp.int32, (DEVICES, DEVICES), 1)
    earlier = (wide == wide.T) & (before < after)
    return jnp.sum(jnp.where(earlier, 1.0, 0.0), axis=0, keepdims=True)


def site_requests(block, cell, frac):
    slot = site_slots(block)
    row, column = cell[0:1], cell[1:2]
    column_next = (column + 1) & (GRID - 1)
    part_row, part_col = frac[0:1], frac[1:2]
    edge = row == ROWS - 1
    tile = (column >> 7).astype(jnp.float32)
    tile_next = (column_next >> 7).astype(jnp.float32)
    line = row.astype(jnp.float32)
    lane = (column & 127).astype(jnp.float32)
    lane_next = (column_next & 127).astype(jnp.float32)
    lower = jnp.where(edge, 0.0, part_row)
    own = [
        PITCH * tile + line,
        PITCH * tile_next + line,
        lane,
        lane_next,
        (1 - part_row) * (1 - part_col),
        (1 - part_row) * part_col,
        lower * (1 - part_col),
        lower * part_col,
    ]
    halo = [
        tile,
        tile_next,
        lane,
        lane_next,
        part_row * (1 - part_col),
        part_row * part_col,
    ]
    blank = jnp.zeros((1, DEVICES), jnp.float32)
    groups = []
    for at, values in ((0, own), (8, own), (16, halo), (22, halo)):
        lines = [blank] * at + values
        groups.append(jnp.concatenate(lines + [blank] * (DEVICES - len(lines)), axis=0))
    owner = lax.broadcasted_iota(jnp.int32, (DEVICES, DEVICES), 0)
    here = owner == block
    below = (owner == ((block + 1) & (DEVICES - 1))) & edge
    picks = []
    for mask in (here, below):
        for which in (0.0, 1.0):
            picks.append(jnp.where(mask & (slot == which), 1.0, 0.0))
    return lax.dot_general(
        jnp.concatenate(picks, axis=1),
        jnp.concatenate(groups, axis=1),
        LAST,
        precision=HIGH,
        preferred_element_type=jnp.float32,
    )


def first_kernel(
    noise_hbm,
    power_hbm,
    block_hbm,
    cell_hbm,
    frac_hbm,
    short_hbm,
    turn_hbm,
    long_hbm,
    out_ref,
    noise,
    power,
    block_ref,
    cell_ref,
    frac_ref,
    short_ref,
    turn_ref,
    long_ref,
    middle,
    noise_sem,
    power_sem,
    small_sem,
):
    small = [
        pltpu.make_async_copy(source, target, small_sem.at[k])
        for k, (source, target) in enumerate(
            (
                (block_hbm, block_ref),
                (cell_hbm, cell_ref),
                (frac_hbm, frac_ref),
                (short_hbm, short_ref),
                (turn_hbm, turn_ref),
                (long_hbm, long_ref),
            )
        )
    ]
    large = []
    for k, (start, count) in enumerate(CHUNKS):
        span = pl.ds(start, count)
        large.append(
            (
                pltpu.make_async_copy(power_hbm.at[span], power.at[span], power_sem.at[k]),
                pltpu.make_async_copy(noise_hbm.at[:, span], noise.at[:, span], noise_sem.at[k]),
            )
        )
    for copy in small[:5] + list(large[0]) + small[5:]:
        copy.start()
    for pair in large[1:]:
        pair[0].start()
        pair[1].start()
    for copy in small[:3]:
        copy.wait()
    out_ref[pl.ds(MESSAGE - 1, DEVICES, stride=MESSAGE), :] = site_requests(
        block_ref[...], cell_ref[...], frac_ref[...]
    )
    small[3].wait()
    small[4].wait()
    for k, (start, count) in enumerate(CHUNKS):
        large[k][0].wait()
        large[k][1].wait()
        for first in range(8 * start, 8 * (start + count), 2):
            parts = []
            for row in (first, first + 1):
                at = pl.ds(row % 8, 64, stride=8)
                level = power[row // 8, at, :]
                amplitude = level * lax.rsqrt(level)
                stacked = jnp.concatenate(
                    [amplitude * noise[0, row // 8, at, :], amplitude * noise[1, row // 8, at, :]],
                    axis=0,
                )
                parts.append(jnp.concatenate(split(stacked), axis=0))
            sums = dot(short_ref[...], jnp.concatenate(parts, axis=1))
            sums = sums[:128] + sums[128:]
            for k2 in range(2):
                real = sums[:64, 128 * k2 : 128 * k2 + 128]
                imag = sums[64:, 128 * k2 : 128 * k2 + 128]
                at = pl.ds(first + k2, 64, stride=PITCH)
                middle[0, at, :] = real * turn_ref[0] - imag * turn_ref[1]
                middle[1, at, :] = real * turn_ref[1] + imag * turn_ref[0]
    small[5].wait()
    for step in range(16):
        value = jnp.concatenate(
            [
                jnp.concatenate(
                    [middle[part, pl.ds(PITCH * (4 * step + k), 64), :] for k in range(4)], axis=0
                )
                for part in range(2)
            ],
            axis=1,
        )
        sums = split_dot(long_ref, value, LAST)
        for part in range(2):
            for k in range(2):
                j = 32 * part + 2 * step + k
                out_ref[pl.ds(j, DEVICES, stride=MESSAGE), :] = sums[
                    128 * part : 128 * part + 128, 128 * k : 128 * k + 128
                ]


def second_kernel(
    got_ref,
    long_ref,
    turn_ref,
    short_ref,
    field_hbm,
    answer_ref,
    tiles,
    field,
    picked,
    code_vmem,
    code_smem,
    field_sem,
    code_sem,
):
    for part in range(2):
        field[part, pl.ds(ROWS, 64, stride=PITCH), :] = jnp.zeros((64, 128), jnp.float32)
    asked = got_ref[pl.ds(MESSAGE - 1, DEVICES, stride=MESSAGE), :]
    code_vmem[...] = (asked + 0.5).astype(jnp.int32)
    code_copy = pltpu.make_async_copy(code_vmem, code_smem, code_sem)
    code_copy.start()
    copies = []
    for i in range(8):
        for half in range(2):
            pair = 4 * i + 2 * half
            value = jnp.concatenate(
                [
                    jnp.concatenate(
                        [
                            got_ref[pl.ds(32 * part + pair + k, DEVICES, stride=MESSAGE), :]
                            for k in range(2)
                        ],
                        axis=1,
                    )
                    for part in range(2)
                ],
                axis=0,
            )
            sums = split_dot(long_ref, value)
            turned = []
            for k in range(2):
                real = sums[:128, 128 * k : 128 * k + 128]
                imag = sums[128:, 128 * k : 128 * k + 128]
                turned.append(
                    jnp.concatenate(
                        [
                            real * turn_ref[0] - imag * turn_ref[1],
                            real * turn_ref[1] + imag * turn_ref[0],
                        ],
                        axis=1,
                    )
                )
            sums = split_dot(short_ref, jnp.concatenate(turned, axis=0), LAST)
            for part in range(2):
                for odd in range(2):
                    for k in range(2):
                        top = 128 * part + 64 * odd
                        row = 4 * half + 2 * k + odd
                        value = sums[top : top + 64, 128 * k : 128 * k + 128]
                        tiles[part, pl.ds(512 * i + row, 64, stride=8), :] = value
                        field[part, pl.ds(8 * i + row, 64, stride=PITCH), :] = value
        copies.append(
            pltpu.make_async_copy(
                tiles.at[:, pl.ds(512 * i, 512)], field_hbm.at[:, i], field_sem.at[i]
            )
        )
        copies[-1].start()
    lanes = lax.broadcasted_iota(jnp.int32, (DEVICES, 128), 1).astype(jnp.float32)
    answer = jnp.zeros((DEVICES, 128), jnp.float32)

    def column(at):
        return asked[:, at : at + 1]

    first_row = pl.ds(0, 64, stride=PITCH)
    terms = split(jnp.concatenate([field[0, first_row, :], field[1, first_row, :]], axis=1))
    places = lax.broadcasted_iota(jnp.int32, (DEVICES, 128), 1) & 63
    places = places.astype(jnp.float32)
    masks = [
        jnp.where(places == column(16 + 6 * which + k), 1.0, 0.0).astype(jnp.bfloat16)
        for k in range(2)
        for which in range(2)
    ]
    beyond = dot(jnp.concatenate(masks, axis=0), jnp.concatenate(terms, axis=0))

    def weight(lane, value):
        return jnp.where(lanes == column(lane), column(value), 0.0)

    weights = []
    for which in range(2):
        own, halo = 8 * which, 16 + 6 * which
        upper = weight(own + 2, own + 4) + weight(own + 3, own + 5)
        lower = weight(own + 2, own + 6) + weight(own + 3, own + 7)
        weights.append((upper, lower))
        edge, edge_next = weight(halo + 2, halo + 4), weight(halo + 3, halo + 5)
        for part in range(2):
            span = slice(128 * part, 128 * part + 128)
            value = edge * beyond[128 * which : 128 * which + 128, span]
            value += edge_next * beyond[256 + 128 * which : 384 + 128 * which, span]
            answer = jnp.where(
                lanes == 4 + 2 * which + part, jnp.sum(value, axis=1, keepdims=True), answer
            )
    code_copy.wait()

    head = lax.broadcasted_iota(jnp.int32, (2, 128), 1) == 0

    def gather(device, carry):
        for which in range(2):
            line = code_smem[device, 8 * which]
            line_next = code_smem[device, 8 * which + 1]
            for part in range(2):
                picked[which, part, pl.ds(2 * device, 2), :] = jnp.where(
                    head,
                    field[part, pl.ds(line_next, 2), :],
                    field[part, pl.ds(line, 2), :],
                )
        return carry

    lax.fori_loop(0, DEVICES, gather, 0, unroll=8)
    for which in range(2):
        upper, lower = weights[which]
        for part in range(2):
            value = upper * picked[which, part, pl.ds(0, DEVICES, stride=2), :]
            value += lower * picked[which, part, pl.ds(1, DEVICES, stride=2), :]
            answer = jnp.where(
                lanes == 2 * which + part, jnp.sum(value, axis=1, keepdims=True), answer
            )
    answer_ref[...] = answer
    for copy in copies:
        copy.wait()


def last_kernel(answer_ref, block_ref, cell_ref, out_ref):
    block = block_ref[...]
    slot = site_slots(block)
    edge = cell_ref[0:1] == ROWS - 1
    owner = lax.broadcasted_iota(jnp.int32, (DEVICES, DEVICES), 0)
    values = answer_ref[...].T[:8]
    masks = jnp.concatenate([owner == block, owner == ((block + 1) & (DEVICES - 1))], axis=1)
    high, middle = split(values)
    rest = values - high.astype(jnp.float32) - middle.astype(jnp.float32)
    terms = jnp.concatenate([high, middle, rest.astype(jnp.bfloat16)], axis=0)
    sums = dot(terms, jnp.where(masks, 1.0, 0.0).astype(jnp.bfloat16))
    sums = sums[0:8] + sums[8:16] + sums[16:24]
    here, below = sums[:, :DEVICES], sums[:, DEVICES:]
    own = jnp.where(slot == 0.0, here[0:2], here[2:4])
    halo = jnp.where(slot == 0.0, below[4:6], below[6:8])
    out_ref[...] = own + jnp.where(edge, halo, 0.0)


def exchange(value):
    return lax.all_to_all(value, AXES, split_axis=0, concat_axis=0, tiled=True)


def per_device(spectrum_noise, power_spectrum, site_block, site_cell, site_frac):
    short_first, turn_first, long_both, turn_second, short_second = make_tables()
    any_space = pl.BlockSpec(memory_space=pl.ANY)
    noise = spectrum_noise.reshape(2, 8, 8, 64, 128).transpose(0, 1, 3, 2, 4).reshape(2, 8, 512, 128)
    power = power_spectrum.reshape(8, 8, 64, 128).transpose(0, 2, 1, 3).reshape(8, 512, 128)
    block = site_block.reshape(1, DEVICES)
    operands = [
        pltpu.with_memory_space_constraint(operand, pltpu.HBM)
        for operand in map(
            jnp.asarray,
            (noise, power, block, site_cell, site_frac, short_first, turn_first, long_both),
        )
    ]
    sent = pl.pallas_call(
        first_kernel,
        out_shape=jax.ShapeDtypeStruct((DEVICES * MESSAGE, 128), jnp.float32),
        in_specs=[pl.BlockSpec(memory_space=pltpu.HBM)] * 8,
        out_specs=VMEM,
        scratch_shapes=[
            pltpu.VMEM((2, 8, 512, 128), jnp.float32),
            pltpu.VMEM((8, 512, 128), jnp.float32),
            pltpu.VMEM((1, DEVICES), jnp.int32),
            pltpu.VMEM((2, DEVICES), jnp.int32),
            pltpu.VMEM((2, DEVICES), jnp.float32),
            pltpu.VMEM((256, 256), jnp.bfloat16),
            pltpu.VMEM((2, 64, 128), jnp.float32),
            pltpu.VMEM((2, 256, 256), jnp.bfloat16),
            pltpu.VMEM((2, 64 * PITCH, 128), jnp.float32),
            pltpu.SemaphoreType.DMA((len(CHUNKS),)),
            pltpu.SemaphoreType.DMA((len(CHUNKS),)),
            pltpu.SemaphoreType.DMA((6,)),
        ],
        compiler_params=pltpu.CompilerParams(vmem_limit_bytes=40 << 20),
        name="first_pass",
    )(*operands)
    got = exchange(sent.reshape(DEVICES * MESSAGE, 1, 128)).reshape(DEVICES * MESSAGE, 128)
    field, answer = pl.pallas_call(
        second_kernel,
        out_shape=(
            jax.ShapeDtypeStruct((2, 8, 512, 128), jnp.float32),
            jax.ShapeDtypeStruct((DEVICES, 128), jnp.float32),
        ),
        in_specs=[VMEM] * 4,
        out_specs=(any_space, VMEM),
        scratch_shapes=[
            pltpu.VMEM((2, 4096, 128), jnp.float32),
            pltpu.VMEM((2, 64 * PITCH, 128), jnp.float32),
            pltpu.VMEM((2, 2, 2 * DEVICES, 128), jnp.float32),
            pltpu.VMEM((DEVICES, 128), jnp.int32),
            pltpu.SMEM((DEVICES, 128), jnp.int32),
            pltpu.SemaphoreType.DMA((8,)),
            pltpu.SemaphoreType.DMA,
        ],
        compiler_params=pltpu.CompilerParams(vmem_limit_bytes=40 << 20),
        name="second_pass",
    )(got, long_both, turn_second, short_second)
    back = exchange(answer.reshape(DEVICES, 1, 128)).reshape(DEVICES, 128)
    samples = pl.pallas_call(
        last_kernel,
        out_shape=jax.ShapeDtypeStruct((2, DEVICES), jnp.float32),
        in_specs=[VMEM] * 3,
        out_specs=VMEM,
        name="samples",
    )(back, block, site_cell)
    field = field.reshape(2, 8, 64, 8, 128).transpose(0, 1, 3, 2, 4).reshape(2, ROWS, GRID)
    return field, samples


def solution(mesh):
    return jax.shard_map(
        per_device,
        mesh=mesh,
        in_specs=(
            P(None, AXES, None),
            P(AXES, None),
            P(AXES),
            P(None, AXES),
            P(None, AXES),
        ),
        out_specs=(P(None, AXES, None), P(None, AXES)),
        check_vma=False,
    )
```

```python
import numpy as np
import ml_dtypes
import jax
import jax.numpy as jnp
from jax import lax
from jax.experimental import pallas as pl
from jax.experimental.pallas import tpu as pltpu
from jax.sharding import PartitionSpec as P

GRID = 8192
DEVICES = 128
ROWS = 64
MESSAGE = 65
PITCH = 72
CHUNKS = ((0, 2), (2, 3), (5, 3))
AXES = ("row", "col")
VMEM = pl.BlockSpec(memory_space=pltpu.VMEM)
HIGH = lax.Precision.HIGHEST
LAST = (((1,), (1,)), ((), ()))


def phase(product, length):
    angle = 2.0 * np.pi / length * (product % length)
    return np.cos(angle), np.sin(angle)


def complex_matrix(cosine, sine):
    return np.block([[cosine, -sine], [sine, cosine]])


def split_table(table):
    high = table.astype(ml_dtypes.bfloat16)
    low = (table - high.astype(np.float64)).astype(ml_dtypes.bfloat16)
    return high, low


def make_tables():
    short, long = np.arange(64), np.arange(128)
    high, low = split_table(complex_matrix(*phase(np.outer(short, short), 64)))
    short_first = np.block([[high, high], [low, np.zeros_like(low)]])
    turn_first = np.stack(phase(np.outer(short, long), GRID)).astype(np.float32)
    long_both = np.stack(split_table(complex_matrix(*phase(np.outer(long, long), 128))))
    turn_second = np.stack(phase(np.outer(long, short), GRID)) / GRID
    turn_second = np.concatenate([turn_second, turn_second], axis=2).astype(np.float32)
    cosine, sine = phase(np.outer(short, short), 64)
    pair = np.eye(2)
    short_second = np.stack(
        split_table(complex_matrix(np.kron(pair, cosine), np.kron(pair, sine)))
    )
    return short_first, turn_first, long_both, turn_second, short_second


def split(value):
    high = value.astype(jnp.bfloat16)
    low = (value - high.astype(jnp.float32)).astype(jnp.bfloat16)
    return high, low


def dot(left, right, dims=(((1,), (0,)), ((), ()))):
    return lax.dot_general(left, right, dims, preferred_element_type=jnp.float32)


def split_dot(table, value, dims=(((1,), (0,)), ((), ()))):
    high, low = split(value)
    return dot(table[0], low, dims) + dot(table[1], high, dims) + dot(table[0], high, dims)


def site_slots(block):
    wide = jnp.broadcast_to(block.astype(jnp.float32), (DEVICES, DEVICES))
    before = lax.broadcasted_iota(jnp.int32, (DEVICES, DEVICES), 0)
    after = lax.broadcasted_iota(jnp.int32, (DEVICES, DEVICES), 1)
    earlier = (wide == wide.T) & (before < after)
    return jnp.sum(jnp.where(earlier, 1.0, 0.0), axis=0, keepdims=True)


def site_requests(block, cell, frac):
    slot = site_slots(block)
    row, column = cell[0:1], cell[1:2]
    column_next = (column + 1) & (GRID - 1)
    part_row, part_col = frac[0:1], frac[1:2]
    edge = row == ROWS - 1
    tile = (column >> 7).astype(jnp.float32)
    tile_next = (column_next >> 7).astype(jnp.float32)
    line = row.astype(jnp.float32)
    lane = (column & 127).astype(jnp.float32)
    lane_next = (column_next & 127).astype(jnp.float32)
    lower = jnp.where(edge, 0.0, part_row)
    own = [
        PITCH * tile + line,
        PITCH * tile_next + line,
        lane,
        lane_next,
        (1 - part_row) * (1 - part_col),
        (1 - part_row) * part_col,
        lower * (1 - part_col),
        lower * part_col,
    ]
    halo = [
        tile,
        tile_next,
        lane,
        lane_next,
        part_row * (1 - part_col),
        part_row * part_col,
    ]
    blank = jnp.zeros((1, DEVICES), jnp.float32)
    groups = []
    for at, values in ((0, own), (8, own), (16, halo), (22, halo)):
        lines = [blank] * at + values
        groups.append(jnp.concatenate(lines + [blank] * (DEVICES - len(lines)), axis=0))
    owner = lax.broadcasted_iota(jnp.int32, (DEVICES, DEVICES), 0)
    here = owner == block
    below = (owner == ((block + 1) & (DEVICES - 1))) & edge
    picks = []
    for mask in (here, below):
        for which in (0.0, 1.0):
            picks.append(jnp.where(mask & (slot == which), 1.0, 0.0))
    return lax.dot_general(
        jnp.concatenate(picks, axis=1),
        jnp.concatenate(groups, axis=1),
        LAST,
        precision=HIGH,
        preferred_element_type=jnp.float32,
    )


def first_kernel(
    noise_hbm,
    power_hbm,
    block_hbm,
    cell_hbm,
    frac_hbm,
    short_hbm,
    turn_hbm,
    long_hbm,
    out_ref,
    noise,
    power,
    block_ref,
    cell_ref,
    frac_ref,
    short_ref,
    turn_ref,
    long_ref,
    middle,
    noise_sem,
    power_sem,
    small_sem,
):
    small = [
        pltpu.make_async_copy(source, target, small_sem.at[k])
        for k, (source, target) in enumerate(
            (
                (block_hbm, block_ref),
                (cell_hbm, cell_ref),
                (frac_hbm, frac_ref),
                (short_hbm, short_ref),
                (turn_hbm, turn_ref),
                (long_hbm, long_ref),
            )
        )
    ]
    large = []
    for k, (start, count) in enumerate(CHUNKS):
        span = pl.ds(start, count)
        large.append(
            (
                pltpu.make_async_copy(power_hbm.at[span], power.at[span], power_sem.at[k]),
                pltpu.make_async_copy(noise_hbm.at[:, span], noise.at[:, span], noise_sem.at[k]),
            )
        )
    for copy in small[:5] + list(large[0]) + small[5:]:
        copy.start()
    for pair in large[1:]:
        pair[0].start()
        pair[1].start()
    for copy in small[:3]:
        copy.wait()
    out_ref[pl.ds(MESSAGE - 1, DEVICES, stride=MESSAGE), :] = site_requests(
        block_ref[...], cell_ref[...], frac_ref[...]
    )
    small[3].wait()
    small[4].wait()
    for k, (start, count) in enumerate(CHUNKS):
        large[k][0].wait()
        large[k][1].wait()
        for first in range(8 * start, 8 * (start + count), 2):
            parts = []
            for row in (first, first + 1):
                at = pl.ds(row % 8, 64, stride=8)
                level = power[row // 8, at, :]
                amplitude = level * lax.rsqrt(level)
                stacked = jnp.concatenate(
                    [amplitude * noise[0, row // 8, at, :], amplitude * noise[1, row // 8, at, :]],
                    axis=0,
                )
                parts.append(jnp.concatenate(split(stacked), axis=0))
            sums = dot(short_ref[...], jnp.concatenate(parts, axis=1))
            sums = sums[:128] + sums[128:]
            for k2 in range(2):
                real = sums[:64, 128 * k2 : 128 * k2 + 128]
                imag = sums[64:, 128 * k2 : 128 * k2 + 128]
                at = pl.ds(first + k2, 64, stride=PITCH)
                middle[0, at, :] = real * turn_ref[0] - imag * turn_ref[1]
                middle[1, at, :] = real * turn_ref[1] + imag * turn_ref[0]
    small[5].wait()
    for step in range(16):
        value = jnp.concatenate(
            [
                jnp.concatenate(
                    [middle[part, pl.ds(PITCH * (4 * step + k), 64), :] for k in range(4)], axis=0
                )
                for part in range(2)
            ],
            axis=1,
        )
        sums = split_dot(long_ref, value, LAST)
        for part in range(2):
            for k in range(2):
                j = 32 * part + 2 * step + k
                out_ref[pl.ds(j, DEVICES, stride=MESSAGE), :] = sums[
                    128 * part : 128 * part + 128, 128 * k : 128 * k + 128
                ]


def second_kernel(
    got_ref,
    long_ref,
    turn_ref,
    short_ref,
    field_hbm,
    answer_ref,
    tiles,
    field,
    picked,
    code_vmem,
    code_smem,
    field_sem,
    code_sem,
):
    for part in range(2):
        field[part, pl.ds(ROWS, 64, stride=PITCH), :] = jnp.zeros((64, 128), jnp.float32)
    asked = got_ref[pl.ds(MESSAGE - 1, DEVICES, stride=MESSAGE), :]
    code_vmem[...] = (asked + 0.5).astype(jnp.int32)
    code_copy = pltpu.make_async_copy(code_vmem, code_smem, code_sem)
    code_copy.start()
    copies = []
    for i in range(8):
        for half in range(2):
            pair = 4 * i + 2 * half
            value = jnp.concatenate(
                [
                    jnp.concatenate(
                        [
                            got_ref[pl.ds(32 * part + pair + k, DEVICES, stride=MESSAGE), :]
                            for k in range(2)
                        ],
                        axis=1,
                    )
                    for part in range(2)
                ],
                axis=0,
            )
            sums = split_dot(long_ref, value)
            turned = []
            for k in range(2):
                real = sums[:128, 128 * k : 128 * k + 128]
                imag = sums[128:, 128 * k : 128 * k + 128]
                turned.append(
                    jnp.concatenate(
                        [
                            real * turn_ref[0] - imag * turn_ref[1],
                            real * turn_ref[1] + imag * turn_ref[0],
                        ],
                        axis=1,
                    )
                )
            sums = split_dot(short_ref, jnp.concatenate(turned, axis=0), LAST)
            for part in range(2):
                for odd in range(2):
                    for k in range(2):
                        top = 128 * part + 64 * odd
                        row = 4 * half + 2 * k + odd
                        value = sums[top : top + 64, 128 * k : 128 * k + 128]
                        tiles[part, pl.ds(512 * i + row, 64, stride=8), :] = value
                        field[part, pl.ds(8 * i + row, 64, stride=PITCH), :] = value
        copies.append(
            pltpu.make_async_copy(
                tiles.at[:, pl.ds(512 * i, 512)], field_hbm.at[:, i], field_sem.at[i]
            )
        )
        copies[-1].start()
    lanes = lax.broadcasted_iota(jnp.int32, (DEVICES, 128), 1).astype(jnp.float32)
    answer = jnp.zeros((DEVICES, 128), jnp.float32)

    def column(at):
        return asked[:, at : at + 1]

    first_row = pl.ds(0, 64, stride=PITCH)
    terms = split(jnp.concatenate([field[0, first_row, :], field[1, first_row, :]], axis=1))
    places = lax.broadcasted_iota(jnp.int32, (DEVICES, 128), 1) & 63
    places = places.astype(jnp.float32)
    masks = [
        jnp.where(places == column(16 + 6 * which + k), 1.0, 0.0).astype(jnp.bfloat16)
        for k in range(2)
        for which in range(2)
    ]
    beyond = dot(jnp.concatenate(masks, axis=0), jnp.concatenate(terms, axis=0))

    def weight(lane, value):
        return jnp.where(lanes == column(lane), column(value), 0.0)

    weights = []
    for which in range(2):
        own, halo = 8 * which, 16 + 6 * which
        upper = weight(own + 2, own + 4) + weight(own + 3, own + 5)
        lower = weight(own + 2, own + 6) + weight(own + 3, own + 7)
        weights.append((upper, lower))
        edge, edge_next = weight(halo + 2, halo + 4), weight(halo + 3, halo + 5)
        for part in range(2):
            span = slice(128 * part, 128 * part + 128)
            value = edge * beyond[128 * which : 128 * which + 128, span]
            value += edge_next * beyond[256 + 128 * which : 384 + 128 * which, span]
            answer = jnp.where(
                lanes == 4 + 2 * which + part, jnp.sum(value, axis=1, keepdims=True), answer
            )
    code_copy.wait()

    head = lax.broadcasted_iota(jnp.int32, (2, 128), 1) == 0

    def gather(device, carry):
        for which in range(2):
            line = code_smem[device, 8 * which]
            line_next = code_smem[device, 8 * which + 1]
            for part in range(2):
                picked[which, part, pl.ds(2 * device, 2), :] = jnp.where(
                    head,
                    field[part, pl.ds(line_next, 2), :],
                    field[part, pl.ds(line, 2), :],
                )
        return carry

    lax.fori_loop(0, DEVICES, gather, 0, unroll=32)
    for which in range(2):
        upper, lower = weights[which]
        for part in range(2):
            value = upper * picked[which, part, pl.ds(0, DEVICES, stride=2), :]
            value += lower * picked[which, part, pl.ds(1, DEVICES, stride=2), :]
            answer = jnp.where(
                lanes == 2 * which + part, jnp.sum(value, axis=1, keepdims=True), answer
            )
    answer_ref[...] = answer
    for copy in copies:
        copy.wait()


def last_kernel(answer_ref, block_ref, cell_ref, out_ref):
    block = block_ref[...]
    slot = site_slots(block)
    edge = cell_ref[0:1] == ROWS - 1
    owner = lax.broadcasted_iota(jnp.int32, (DEVICES, DEVICES), 0)
    values = answer_ref[...].T[:8]
    masks = jnp.concatenate([owner == block, owner == ((block + 1) & (DEVICES - 1))], axis=1)
    high, middle = split(values)
    rest = values - high.astype(jnp.float32) - middle.astype(jnp.float32)
    terms = jnp.concatenate([high, middle, rest.astype(jnp.bfloat16)], axis=0)
    sums = dot(terms, jnp.where(masks, 1.0, 0.0).astype(jnp.bfloat16))
    sums = sums[0:8] + sums[8:16] + sums[16:24]
    here, below = sums[:, :DEVICES], sums[:, DEVICES:]
    own = jnp.where(slot == 0.0, here[0:2], here[2:4])
    halo = jnp.where(slot == 0.0, below[4:6], below[6:8])
    out_ref[...] = own + jnp.where(edge, halo, 0.0)


def exchange(value):
    return lax.all_to_all(value, AXES, split_axis=0, concat_axis=0, tiled=True)


def per_device(spectrum_noise, power_spectrum, site_block, site_cell, site_frac):
    short_first, turn_first, long_both, turn_second, short_second = make_tables()
    any_space = pl.BlockSpec(memory_space=pl.ANY)
    noise = spectrum_noise.reshape(2, 8, 8, 64, 128).transpose(0, 1, 3, 2, 4).reshape(2, 8, 512, 128)
    power = power_spectrum.reshape(8, 8, 64, 128).transpose(0, 2, 1, 3).reshape(8, 512, 128)
    block = site_block.reshape(1, DEVICES)
    operands = [
        pltpu.with_memory_space_constraint(operand, pltpu.HBM)
        for operand in map(
            jnp.asarray,
            (noise, power, block, site_cell, site_frac, short_first, turn_first, long_both),
        )
    ]
    sent = pl.pallas_call(
        first_kernel,
        out_shape=jax.ShapeDtypeStruct((DEVICES * MESSAGE, 128), jnp.float32),
        in_specs=[pl.BlockSpec(memory_space=pltpu.HBM)] * 8,
        out_specs=VMEM,
        scratch_shapes=[
            pltpu.VMEM((2, 8, 512, 128), jnp.float32),
            pltpu.VMEM((8, 512, 128), jnp.float32),
            pltpu.VMEM((1, DEVICES), jnp.int32),
            pltpu.VMEM((2, DEVICES), jnp.int32),
            pltpu.VMEM((2, DEVICES), jnp.float32),
            pltpu.VMEM((256, 256), jnp.bfloat16),
            pltpu.VMEM((2, 64, 128), jnp.float32),
            pltpu.VMEM((2, 256, 256), jnp.bfloat16),
            pltpu.VMEM((2, 64 * PITCH, 128), jnp.float32),
            pltpu.SemaphoreType.DMA((len(CHUNKS),)),
            pltpu.SemaphoreType.DMA((len(CHUNKS),)),
            pltpu.SemaphoreType.DMA((6,)),
        ],
        compiler_params=pltpu.CompilerParams(vmem_limit_bytes=40 << 20),
        name="first_pass",
    )(*operands)
    got = exchange(sent.reshape(DEVICES * MESSAGE, 1, 128)).reshape(DEVICES * MESSAGE, 128)
    field, answer = pl.pallas_call(
        second_kernel,
        out_shape=(
            jax.ShapeDtypeStruct((2, 8, 512, 128), jnp.float32),
            jax.ShapeDtypeStruct((DEVICES, 128), jnp.float32),
        ),
        in_specs=[VMEM] * 4,
        out_specs=(any_space, VMEM),
        scratch_shapes=[
            pltpu.VMEM((2, 4096, 128), jnp.float32),
            pltpu.VMEM((2, 64 * PITCH, 128), jnp.float32),
            pltpu.VMEM((2, 2, 2 * DEVICES, 128), jnp.float32),
            pltpu.VMEM((DEVICES, 128), jnp.int32),
            pltpu.SMEM((DEVICES, 128), jnp.int32),
            pltpu.SemaphoreType.DMA((8,)),
            pltpu.SemaphoreType.DMA,
        ],
        compiler_params=pltpu.CompilerParams(vmem_limit_bytes=40 << 20),
        name="second_pass",
    )(got, long_both, turn_second, short_second)
    back = exchange(answer.reshape(DEVICES, 1, 128)).reshape(DEVICES, 128)
    samples = pl.pallas_call(
        last_kernel,
        out_shape=jax.ShapeDtypeStruct((2, DEVICES), jnp.float32),
        in_specs=[VMEM] * 3,
        out_specs=VMEM,
        name="samples",
    )(back, block, site_cell)
    field = field.reshape(2, 8, 64, 8, 128).transpose(0, 1, 3, 2, 4).reshape(2, ROWS, GRID)
    return field, samples


def solution(mesh):
    return jax.shard_map(
        per_device,
        mesh=mesh,
        in_specs=(
            P(None, AXES, None),
            P(AXES, None),
            P(AXES),
            P(None, AXES),
            P(None, AXES),
        ),
        out_specs=(P(None, AXES, None), P(None, AXES)),
        check_vma=False,
    )
```
